32 devices in a mesh: slab: 8 (over z, y), snap: 4 (over x, core).
Axes of the slice: x: 2, y: 2, z: 4, core: 2. Of those that a mesh axis runs over, the one named last changes fastest.
Arguments:
- flow: bfloat16 [64, 3, 16, 64, 128], P('snap', None, 'slab'), may hold values from -127 to 127
- large_scale: bfloat16 [3, 16, 64, 128], P(None, 'slab'), may hold values from -6 to 6
- modulation: float32 [64, 64], replicated, may hold values from -15 to 15
- metric: float32 [4, 16, 64, 128], P(None, 'slab'), may hold values from -0.5 to 9.6
Outputs:
- whitened: float32 [64, 3, 16, 64, 128], P(None, None, 'slab', 'snap')
The draws below stay inside these ranges and needn't reach their ends.
All inputs are finite; a program needn't handle non-finite values.
Results may differ from the reference program's by a relative error of at most 0.0003.
Values may be sent and summed in bfloat16 or wider, within the bound.
No kernel may reach another device: no remote copies, remote signals or barrier semaphores. Data moves between devices by JAX's collectives and lax.ppermute only.
A program may use at most 64 MiB of HBM per device.

```python
import math
import jax
import jax.numpy as jnp
from jax import lax

NX = 64
NZ = 128
NSITER = 6
S = 64
NY = 16


def draw_flow(key, part):
    key_base, key_snap, key_plane = jax.random.split(key, 3)
    shape_all = (S, 3, NY, NX, NZ)
    base = jax.random.truncated_normal(key_base, -4.0, 4.0, shape_all, jnp.float32)
    snap_scale = jnp.exp(jax.random.uniform(key_snap, (S,), jnp.float32) * math.log(10.0))
    plane_scale = jnp.exp(jax.random.uniform(key_plane, (NY,), jnp.float32) * (0.5 * math.log(10.0)))
    values = base * snap_scale[:, None, None, None, None] * plane_scale[None, None, :, None, None]
    return values.astype(jnp.bfloat16)


def draw_metric(key, part):
    key_x, key_shear, key_y, key_z = jax.random.split(key, 4)
    shape_cells = (NY, NX, NZ)
    planes_pos = jnp.arange(NY).astype(jnp.float32) / max(NY - 1, 1)
    stretch = 1.0 + 3.0 * planes_pos
    metric_x = jax.random.uniform(key_x, shape_cells, jnp.float32, 0.6, 1.6)
    shear_xy = jax.random.uniform(key_shear, shape_cells, jnp.float32, -0.5, 0.5)
    metric_y = stretch[:, None, None] * jax.random.uniform(key_y, shape_cells, jnp.float32, 0.6, 1.6)
    metric_z = jax.random.uniform(key_z, shape_cells, jnp.float32, 0.6, 1.6)
    return jnp.stack([metric_x, shear_xy, metric_y, metric_z], axis=0)


def shard_levels(key, shape, cuts, smallest, high):
    def one(position, shards_of):
        draws = jax.random.uniform(jax.random.fold_in(jax.random.fold_in(key, 6), position), (shards_of,), jnp.float32, smallest / len(cuts), high / len(cuts))
        return jnp.repeat(jnp.exp(draws), shape[position] // shards_of).reshape((-1,) + (1,) * (len(shape) - position - 1))

    level = one(*cuts[0])
    for cut in cuts[1:]:
        level = level * one(*cut)
    return level


def gaussian(key, shape, width, limit, cuts=(), kind=jnp.bfloat16):
    factor_of = shard_levels(key, shape, cuts, -0.22, 0.18) if cuts else 1.0
    array = jax.random.normal(key, shape, jnp.float32) * width * factor_of
    return jnp.minimum(jnp.maximum(array, -limit), limit).astype(kind)


def setup_inputs(seed: int = 0) -> dict:
    seeds = jax.random.split(jax.random.key(seed), 5)
    flow = draw_flow(jax.random.fold_in(seeds[4], 71), 0)
    large_scale = gaussian(seeds[1], (3, NY, NX, NZ), 1.0, 6.0, ((1, 8),))
    modulation = gaussian(seeds[2], (S, NX), 3.0, 15.0, (), jnp.float32)
    metric = draw_metric(jax.random.fold_in(seeds[4], 71), 0)
    return {"flow": flow, "large_scale": large_scale, "modulation": modulation, "metric": metric}


def vorticity(velocity, metric):
    metric_x = metric[0]
    shear_xy = metric[1]
    metric_y = metric[2]
    metric_z = metric[3]

    def along_x(values):
        return 0.5 * (values[..., 1:-1, 2:, :] - values[..., 1:-1, :-2, :])

    def along_y(values):
        return 0.5 * (values[..., 2:, 1:-1, :] - values[..., :-2, 1:-1, :])

    def along_z(values):
        center = values[..., 1:-1, 1:-1, :]
        return 0.5 * (jnp.roll(center, -1, -1) - jnp.roll(center, 1, -1))

    def slope_x(values):
        return metric_x * along_x(values) + shear_xy * along_y(values)

    def slope_y(values):
        return metric_y * along_y(values)

    def slope_z(values):
        return metric_z * along_z(values)
    stream = velocity[..., 0, :, :, :]
    normal = velocity[..., 1, :, :, :]
    spanwise = velocity[..., 2, :, :, :]
    around_x = slope_y(spanwise) - slope_z(normal)
    around_y = slope_z(stream) - slope_x(spanwise)
    around_z = slope_x(normal) - slope_y(stream)
    return jnp.stack([around_x, around_y, around_z], axis=-4)

def wrap_columns(values):
    return jnp.concatenate([values[..., -1:, :], values, values[..., :1, :]], axis=-2)

def whitening(correlation):
    identity = jnp.eye(correlation.shape[0], dtype=correlation.dtype)
    frob_scale = jnp.sqrt(jnp.sum(correlation * correlation) + 1e-06)
    approx = correlation / frob_scale
    inverse = identity
    for repeat in range(NSITER):
        factor = 0.5 * (3.0 * identity - jnp.dot(inverse, approx, precision=lax.Precision.HIGHEST))
        approx = jnp.dot(approx, factor, precision=lax.Precision.HIGHEST)
        inverse = jnp.dot(factor, inverse, precision=lax.Precision.HIGHEST)
    return inverse / jnp.sqrt(frob_scale)

def reference(flow, large_scale, modulation, metric):
    large_field = large_scale.astype(jnp.float32)

    def single(inputs):
        snapshot, amplitude = inputs
        velocity = snapshot.astype(jnp.float32) + amplitude[None, None, :, None] * large_field
        padded = jnp.pad(velocity, ((0, 0), (1, 1), (0, 0), (0, 0)))
        return vorticity(wrap_columns(padded), metric)
    fields = lax.map(single, (flow, modulation))
    snapshot_rows = fields.reshape(fields.shape[0], -1)
    gram_total = lax.dot_general(snapshot_rows, snapshot_rows, (((1,), (1,)), ((), ())), precision=lax.Precision.HIGHEST, preferred_element_type=jnp.float32)
    correlation = gram_total / snapshot_rows.shape[1]
    weights = whitening(correlation)
    result = jnp.dot(weights, snapshot_rows, precision=lax.Precision.HIGHEST)
    return result.reshape(fields.shape)
```

```python
import functools

import jax
import jax.numpy as jnp
from jax import lax
from jax.experimental import pallas as pl
from jax.experimental.pallas import tpu as pltpu
from jax.sharding import PartitionSpec as P

NSITER = 6
CORES = 2
VMEM_BYTES = 48 * 1024 * 1024


def pack_kernel(chips, planes, cols, where, flow, large, *refs):
    outs, flat = refs[:-1], refs[-1]
    outs = list(outs)
    snaps, width = flow.shape[0], flow.shape[3]
    extra = outs[0].shape[2] - cols
    own = [outs.pop(0) for _ in range(planes)]
    own_edge = outs.pop(0)
    own_other = outs.pop(0)
    away = [[outs.pop(0) for _ in range(planes)] for _ in range(chips - 1)]
    away_edge = [outs.pop(0) for _ in range(chips - 1)]
    chip, core = where[0], where[1]

    def column(col):
        return flat[pl.ds(col, snaps, stride=width), :].astype(jnp.bfloat16)

    def wrapped(col):
        return lax.rem(col + width, width)

    for plane in range(planes):
        for snap in range(snaps):
            flat[pl.ds(snap * width, width), :] = flow[snap, 0, plane].astype(jnp.float32)
        for step in range(chips):
            base = lax.rem(chip + step, chips) * (CORES * cols)
            for part in range(CORES):
                start = base + part * cols
                target = own[plane] if step == 0 else away[step - 1][plane]
                for col in range(cols):
                    target[0, part, col] = column(start + col)
                if step == 0:
                    rows = large[0, plane, pl.ds(pl.multiple_of(start, 8), cols), :]
                    if cols < extra * snaps:
                        rows = jnp.concatenate([rows] * (extra * snaps // cols), axis=0)
                    for piece in range(extra):
                        target[0, part, cols + piece] = rows[piece * snaps : (piece + 1) * snaps]
                else:
                    edge = away_edge[step - 1]
                    edge[0, part, 2 * plane] = column(wrapped(start - 1))
                    edge[0, part, 2 * plane + 1] = column(wrapped(start + cols))
        mine = chip * (CORES * cols) + core * cols
        own_edge[0, 2 * plane] = column(wrapped(mine - 1))
        own_edge[0, 2 * plane + 1] = column(wrapped(mine + cols))
        other = chip * (CORES * cols) + (1 - core) * cols
        for col in range(cols + 2):
            own_other[0, plane, col] = column(wrapped(other + col - 1))


def pack(flow, large, where, chips, cols):
    snaps, comps, planes, width, depth = flow.shape
    extra = -(-cols // snaps)
    kind = flow.dtype
    shapes = [(comps, CORES, cols + extra, snaps, depth)] * planes
    shapes += [(comps, 2 * planes, snaps, depth), (comps, planes, cols + 2, snaps, depth)]
    shapes += [(comps, CORES, cols, snaps, depth)] * (planes * (chips - 1))
    shapes += [(comps, CORES, 2 * planes, snaps, depth)] * (chips - 1)

    def spec(shape):
        tail = len(shape) - 1
        return pl.BlockSpec((1,) + shape[1:], lambda comp: (comp,) + (0,) * tail)

    outs = pl.pallas_call(
        functools.partial(pack_kernel, chips, planes, cols),
        grid=(comps,),
        in_specs=[
            pl.BlockSpec(memory_space=pltpu.SMEM),
            pl.BlockSpec((snaps, 1, planes, width, depth), lambda comp: (0, comp, 0, 0, 0)),
            pl.BlockSpec((1, planes, width, depth), lambda comp: (comp, 0, 0, 0)),
        ],
        out_specs=[spec(shape) for shape in shapes],
        out_shape=[jax.ShapeDtypeStruct(shape, kind) for shape in shapes],
        scratch_shapes=[pltpu.VMEM((snaps * width, depth), jnp.float32)],
        compiler_params=pltpu.CompilerParams(vmem_limit_bytes=VMEM_BYTES),
        name="pack",
    )(where, flow, large)
    outs = list(outs)
    own = [outs.pop(0) for _ in range(planes)]
    own_edge, own_other = outs.pop(0), outs.pop(0)
    away = [[outs.pop(0) for _ in range(planes)] for _ in range(chips - 1)]
    return own, own_edge, own_other, away, outs


def load_field(refs, where, field, wide, sems, chips, planes, cols, snaps):
    refs = list(refs)
    chip, core = where[0], where[1]
    copies = []

    def copy(source, target):
        copies.append(pltpu.make_async_copy(source, target, sems.at[0]))

    def rows(step, part):
        owner = lax.rem(chip + chips - step, chips) * CORES + part
        return pl.ds(pl.multiple_of(owner * snaps, snaps), snaps)

    own = [refs.pop(0) for _ in range(planes)]
    own_edge, own_other = refs.pop(0), refs.pop(0)
    own_low, own_high, own_low_other, own_high_other = [refs.pop(0) for _ in range(4)]
    mine, theirs = rows(0, core), rows(0, 1 - core)
    middle = pl.ds(1, cols)
    for plane in range(planes):
        copy(own[plane].at[:, core, pl.ds(0, cols)], field.at[:, plane + 1, middle, mine])
        copy(own_edge.at[:, 2 * plane], field.at[:, plane + 1, 0, mine])
        copy(own_edge.at[:, 2 * plane + 1], field.at[:, plane + 1, cols + 1, mine])
        copy(own_other.at[:, plane], field.at[:, plane + 1, :, theirs])
    for target, near, far in ((0, own_low, own_low_other), (planes + 1, own_high, own_high_other)):
        copy(near.at[:, core, pl.ds(0, cols)], field.at[:, target, middle, mine])
        copy(far.at[:, pl.ds(0, cols)], field.at[:, target, middle, theirs])
    extra = wide.shape[2]
    copy(own_low.at[:, core, pl.ds(cols, extra)], wide.at[0])
    copy(own_high.at[:, core, pl.ds(cols, extra)], wide.at[1])
    for step in range(1, chips):
        mine, theirs = rows(step, core), rows(step, 1 - core)
        for plane in range(planes):
            near, far = refs.pop(0), refs.pop(0)
            copy(near.at[:, core], field.at[:, plane + 1, middle, mine])
            copy(far, field.at[:, plane + 1, middle, theirs])
        near, far = refs.pop(0), refs.pop(0)
        for plane in range(planes):
            for side, col in ((0, 0), (1, cols + 1)):
                copy(near.at[:, core, 2 * plane + side], field.at[:, plane + 1, col, mine])
                copy(far.at[:, 2 * plane + side], field.at[:, plane + 1, col, theirs])
        for target in (0, planes + 1):
            near, far = refs.pop(0), refs.pop(0)
            copy(near.at[:, core], field.at[:, target, middle, mine])
            copy(far, field.at[:, target, middle, theirs])
    assert not refs
    for item in copies:
        item.start()
    return copies


def field_kernel(chips, where, metric, large, amplitude, *refs):
    refs, (parts, gram, field, wide, coef, total, sems) = refs[:-7], refs[-7:]
    comps, planes, cols, depth = large.shape[0], metric.shape[1], metric.shape[2], metric.shape[3]
    everyone = field.shape[3]
    snaps = everyone // (chips * CORES)
    for item in load_field(refs, where, field, wide, sems, chips, planes, cols, snaps):
        item.wait()

    def along_z(values):
        return pltpu.roll(values, depth - 1, 1) - pltpu.roll(values, 1, 1)

    def halo(side, comp):
        rows = [wide[side, comp, piece] for piece in range(wide.shape[2])]
        return jnp.concatenate(rows, axis=0).astype(jnp.float32)[:cols]

    for plane in range(planes):
        half_x, half_shear, half_y, half_z = [0.5 * metric[k, plane] for k in range(4)]

        def at(comp, index):
            if index < 0:
                return halo(0, comp)
            if index == planes:
                return halo(1, comp)
            return large[comp, index, 1 : cols + 1]

        step_y = [at(comp, plane + 1) - at(comp, plane - 1) for comp in range(comps)]
        step_z = [along_z(at(comp, plane)) for comp in range(2)]
        after = [large[comp, plane, 2 : cols + 2] for comp in (1, 2)]
        before = [large[comp, plane, 0:cols] for comp in (1, 2)]
        rows = [
            half_x,
            half_shear,
            half_y,
            half_z,
            half_y * step_y[2] - half_z * step_z[1],
            half_z * step_z[0] - half_shear * step_y[2],
            half_shear * step_y[1] - half_y * step_y[0],
            half_x * after[0],
            half_x * before[0],
            half_x * after[1],
            half_x * before[1],
        ]
        for index, value in enumerate(rows):
            coef[plane, index] = value

    total[...] = jnp.zeros_like(total)
    tile = 16
    pairs = cols // 2

    def body(item, carry):
        plane = item // pairs
        first = (item % pairs) * 2
        for sub in range(2):
            col = first + sub
            row = [
                jnp.broadcast_to(coef[plane, index, pl.ds(col, 1), :], (tile, depth))
                for index in range(11)
            ]
            gx, shear, gy, gz, ax, ay, az, v_after, v_before, w_after, w_before = row
            for group in range(everyone // tile):
                span = pl.ds(group * tile, tile)

                def get(comp, plane_at, col_at):
                    return field[comp, plane_at, col_at, span, :].astype(jnp.float32)

                mod_before = amplitude[col, span, :]
                mod_here = amplitude[col + 1, span, :]
                mod_after = amplitude[col + 2, span, :]
                dy_u, dy_v, dy_w = [
                    get(comp, plane + 2, col + 1) - get(comp, plane, col + 1) for comp in range(3)
                ]
                dz_u, dz_v = [along_z(get(comp, plane + 1, col + 1)) for comp in range(2)]
                dx_v, dx_w = [
                    get(comp, plane + 1, col + 2) - get(comp, plane + 1, col) for comp in (1, 2)
                ]
                around_x = gy * dy_w - gz * dz_v + mod_here * ax
                around_y = (
                    gz * dz_u - gx * dx_w - shear * dy_w + mod_here * ay
                    - (mod_after * w_after - mod_before * w_before)
                )
                around_z = (
                    gx * dx_v + shear * dy_v - gy * dy_u + mod_here * az
                    + (mod_after * v_after - mod_before * v_before)
                )
                for comp, value in enumerate((around_x, around_y, around_z)):
                    top = value.astype(jnp.bfloat16)
                    rest = (value - top.astype(jnp.float32)).astype(jnp.bfloat16)
                    parts[comp, plane, col, span, :] = top
                    parts[comp, plane, col, pl.ds(everyone + group * tile, tile), :] = rest
        for comp in range(3):
            both = jnp.concatenate(
                [parts[comp, plane, first], parts[comp, plane, first + 1]], axis=1
            )
            total[...] += lax.dot_general(
                both, both, (((1,), (1,)), ((), ())), preferred_element_type=jnp.float32
            )
        return carry

    lax.fori_loop(0, planes * pairs, body, 0)
    gram[...] = (
        total[:everyone, :everyone]
        + total[everyone:, everyone:]
        + (total[:everyone, everyone:] + total[everyone:, :everyone])
    )


def field_and_gram(where, metric, large, amplitude, arrays, chips, snaps):
    comps = large.shape[0]
    _, planes, cols, depth = metric.shape
    everyone = snaps * chips * CORES
    extra = -(-cols // snaps)
    whole = pl.BlockSpec(memory_space=pltpu.VMEM)
    return pl.pallas_call(
        functools.partial(field_kernel, chips),
        in_specs=[pl.BlockSpec(memory_space=pltpu.SMEM), whole, whole, whole]
        + [pl.BlockSpec(memory_space=pl.ANY)] * len(arrays),
        out_specs=[whole, whole],
        out_shape=[
            jax.ShapeDtypeStruct((comps, planes, cols, 2 * everyone, depth), jnp.bfloat16),
            jax.ShapeDtypeStruct((everyone, everyone), jnp.float32),
        ],
        scratch_shapes=[
            pltpu.VMEM((comps, planes + 2, cols + 2, everyone, depth), jnp.bfloat16),
            pltpu.VMEM((2, comps, extra, snaps, depth), jnp.bfloat16),
            pltpu.VMEM((planes, 11, cols, depth), jnp.float32),
            pltpu.VMEM((2 * everyone, 2 * everyone), jnp.float32),
            pltpu.SemaphoreType.DMA((1,)),
        ],
        compiler_params=pltpu.CompilerParams(vmem_limit_bytes=VMEM_BYTES),
        name="field_and_gram",
    )(where, metric, large, amplitude, *arrays)


def whiten_kernel(count, gram, parts, out, left):
    everyone = gram.shape[0]
    cols = parts.shape[2]

    @pl.when((pl.program_id(0) == 0) & (pl.program_id(1) == 0))
    def _():
        def dot(a, b):
            return jnp.dot(
                a, b, precision=lax.Precision.HIGHEST, preferred_element_type=jnp.float32
            )

        correlation = gram[...] / count
        frob_scale = jnp.sqrt(jnp.sum(correlation * correlation, keepdims=True) + 1e-06)
        approx = correlation / frob_scale
        row = lax.broadcasted_iota(jnp.int32, (everyone, everyone), 0)
        col = lax.broadcasted_iota(jnp.int32, (everyone, everyone), 1)
        diagonal = jnp.where(row == col, 3.0, 0.0)
        factor = 0.5 * (diagonal - approx)
        inverse = factor
        for _ in range(1, NSITER):
            approx = dot(approx, factor)
            factor = 0.5 * (diagonal - dot(inverse, approx))
            inverse = dot(factor, inverse)
        weights = inverse / jnp.sqrt(frob_scale)
        top = weights.astype(jnp.bfloat16)
        rest = (weights - top.astype(jnp.float32)).astype(jnp.bfloat16)
        left[:, :everyone] = top
        left[:, everyone : 2 * everyone] = top
        left[:, 2 * everyone : 3 * everyone] = rest
        left[:, 3 * everyone :] = rest

    depth = out.shape[-1]
    flat = out.reshape(everyone * cols, depth)
    mix = left[...]
    for first in range(0, cols, 2):
        both = jnp.concatenate([parts[0, 0, first], parts[0, 0, first + 1]], axis=1)
        both = jnp.concatenate([both, both], axis=0)
        mixed = jnp.dot(mix, both, preferred_element_type=jnp.float32)
        for sub in range(2):
            flat[pl.ds(first + sub, everyone, stride=cols), :] = mixed[
                :, sub * depth : (sub + 1) * depth
            ]


def whiten(gram, parts, count):
    everyone = gram.shape[0]
    comps, planes, cols, _, depth = parts.shape
    out = pl.pallas_call(
        functools.partial(whiten_kernel, count),
        grid=(comps, planes),
        in_specs=[
            pl.BlockSpec((everyone, everyone), lambda comp, plane: (0, 0)),
            pl.BlockSpec(
                (1, 1, cols, 2 * everyone, depth), lambda comp, plane: (comp, plane, 0, 0, 0)
            ),
        ],
        out_specs=pl.BlockSpec(
            (everyone, 1, 1, cols, depth), lambda comp, plane: (0, comp, plane, 0, 0)
        ),
        out_shape=jax.ShapeDtypeStruct((everyone, comps, planes, cols, depth), jnp.float32),
        scratch_shapes=[pltpu.VMEM((everyone, 4 * everyone), jnp.bfloat16)],
        compiler_params=pltpu.CompilerParams(vmem_limit_bytes=VMEM_BYTES),
        name="whiten",
    )(gram, parts)
    return out


def to_chip(array, step):
    count = lax.axis_size("snap")
    pairs = [(i, (i + step * CORES) % count) for i in range(count)]
    return lax.ppermute(array, "snap", pairs)


def to_core(array):
    return lax.ppermute(array, "snap", [(i, i ^ 1) for i in range(lax.axis_size("snap"))])


def to_slab(array, step):
    count = lax.axis_size("slab")
    pairs = [(i, i + step) for i in range(count) if 0 <= i + step < count]
    return lax.ppermute(array, "slab", pairs)


def all_sum(value):
    for axis in ("snap", "slab"):
        count = lax.axis_size(axis)
        if count & (count - 1):
            value = lax.psum(value, axis)
            continue
        stride = 1
        while stride < count:
            pairs = [(i, i ^ stride) for i in range(count)]
            value = value + lax.ppermute(value, axis, pairs)
            stride *= 2
    return value


def per_device(flow, large_scale, modulation, metric):
    snap_count = lax.axis_size("snap")
    slab_count = lax.axis_size("slab")
    snaps, comps, planes, width, depth = flow.shape
    chips = snap_count // CORES
    cols = width // snap_count
    place = lax.axis_index("snap")
    chip, core = place // CORES, place % CORES
    where = jnp.stack([chip, core]).astype(jnp.int32)

    def half(array, axis):
        return lax.dynamic_index_in_dim(array, 1 - core, axis, keepdims=False)

    own, own_edge, own_other, away, away_edge = pack(flow, large_scale, where, chips, cols)
    own_low = to_slab(own[-1], 1)
    own_high = to_slab(own[0], -1)
    arrays = own + [own_edge, to_core(own_other)]
    arrays += [own_low, own_high, to_core(half(own_low, 1)), to_core(half(own_high, 1))]
    for step in range(1, chips):
        here = [to_chip(item, step) for item in away[step - 1]]
        edge = to_chip(away_edge[step - 1], step)
        low, high = to_slab(here[-1], 1), to_slab(here[0], -1)
        for item in here + [edge, low, high]:
            arrays += [item, to_core(half(item, 1))]

    first = place * cols
    def window(array, axis):
        padded = jnp.concatenate(
            [
                lax.slice_in_dim(array, width - 1, width, axis=axis),
                array,
                lax.slice_in_dim(array, 0, 1, axis=axis),
            ],
            axis=axis,
        )
        return lax.dynamic_slice_in_dim(padded, first, cols + 2, axis)

    large = window(large_scale, 2).astype(jnp.float32)
    amplitude = window(modulation, 1).T[:, :, None]
    amplitude = jnp.broadcast_to(amplitude, amplitude.shape[:2] + (depth,))
    metric_mine = lax.dynamic_slice_in_dim(metric, first, cols, 2)
    parts, gram = field_and_gram(where, metric_mine, large, amplitude, arrays, chips, snaps)
    gram = all_sum(gram)
    return whiten(gram, parts, float(comps * planes * slab_count * width * depth))


def solution(mesh):
    return jax.shard_map(
        per_device,
        mesh=mesh,
        in_specs=(
            P("snap", None, "slab", None, None),
            P(None, "slab", None, None),
            P(),
            P(None, "slab", None, None),
        ),
        out_specs=P(None, None, "slab", "snap", None),
        check_vma=False,
    )
```

```python
import functools

import jax
import jax.numpy as jnp
from jax import lax
from jax.experimental import pallas as pl
from jax.experimental.pallas import tpu as pltpu
from jax.sharding import PartitionSpec as P

NSITER = 6
CORES = 2
VMEM_BYTES = 16 * 1024 * 1024


def whereabouts():
    place = lax.axis_index("snap")
    return lax.div(place, CORES), lax.rem(place, CORES)


def pack_columns(flow, flat, plane):
    snaps, width = flow.shape[0], flow.shape[3]
    pitch = width + 1
    for snap in range(snaps):
        flat[pl.ds(snap * pitch, width), :] = flow[snap, 0, plane].astype(jnp.float32)

    def column(col):
        return flat[pl.ds(col, snaps, stride=pitch), :].astype(jnp.bfloat16)

    return column


def pack_own_kernel(planes, cols, flow, large, *refs):
    own, (flat, near, large_rows, sem) = refs[:-4], refs[-4:]
    snaps = flow.shape[0]
    extra = own[0].shape[2] - cols
    chip, _ = whereabouts()
    comp = pl.program_id(0)
    fetch = pltpu.make_async_copy(large.at[comp], near, sem.at[0])
    fetch.start()
    for plane in range(planes):
        column = pack_columns(flow, flat, plane)
        for part in range(CORES):
            start = chip * (CORES * cols) + part * cols
            for col in range(cols):
                own[plane][0, part, col] = column(start + col)
    fetch.wait()
    large_rows[...] = near[...].astype(jnp.float32)
    for plane in range(planes):
        for part in range(CORES):
            start = chip * (CORES * cols) + part * cols
            rows = large_rows[plane, pl.ds(pl.multiple_of(start, 8), cols), :]
            if cols < extra * snaps:
                rows = jnp.concatenate([rows] * (extra * snaps // cols), axis=0)
            for piece in range(extra):
                tile = rows[piece * snaps : (piece + 1) * snaps]
                own[plane][0, part, cols + piece] = tile.astype(jnp.bfloat16)


def pack_away_kernel(chips, planes, cols, flow, first, *refs):
    outs, flat = list(refs[:-1]), refs[-1]
    width = flow.shape[3]
    own_edge, own_other = outs.pop(0), outs.pop(0)
    mine, other = outs[: chips - 1], outs[chips - 1 :]
    chip, core = whereabouts()
    for plane in range(planes):
        column = pack_columns(flow, flat, plane)

        def window(target, start):
            target[0, plane, 0] = column(lax.rem(start - 1 + width, width))
            for col in range(cols):
                target[0, plane, col + 1] = column(start + col)
            target[0, plane, cols + 1] = column(lax.rem(start + cols, width))

        for step in range(1, chips):
            base = lax.rem(chip + step, chips) * (CORES * cols)
            window(other[step - 1], base + (1 - core) * cols)
            window(mine[step - 1], base + core * cols)
        base = chip * (CORES * cols)
        window(own_other, base + (1 - core) * cols)
        start = base + core * cols
        own_edge[0, 2 * plane] = column(lax.rem(start - 1 + width, width))
        own_edge[0, 2 * plane + 1] = column(lax.rem(start + cols, width))


def pack(flow, large, chips, cols):
    snaps, comps, planes, width, depth = flow.shape
    extra = -(-cols // snaps)

    def spec(shape):
        tail = len(shape) - 1
        return pl.BlockSpec((1,) + shape[1:], lambda comp: (comp,) + (0,) * tail)

    def call(kernel, shapes, second, scratch, name):
        return list(
            pl.pallas_call(
                kernel,
                grid=(comps,),
                in_specs=[
                    pl.BlockSpec((snaps, 1, planes, width, depth), lambda comp: (0, comp, 0, 0, 0)),
                    pl.BlockSpec(memory_space=pl.ANY),
                ],
                out_specs=[spec(shape) for shape in shapes],
                out_shape=[jax.ShapeDtypeStruct(shape, flow.dtype) for shape in shapes],
                scratch_shapes=[pltpu.VMEM((snaps * (width + 1), depth), jnp.float32)] + scratch,
                compiler_params=pltpu.CompilerParams(vmem_limit_bytes=VMEM_BYTES),
                name=name,
            )(flow, second)
        )

    own = call(
        functools.partial(pack_own_kernel, planes, cols),
        [(comps, CORES, cols + extra, snaps, depth)] * planes,
        large,
        [
            pltpu.VMEM((planes, width, depth), large.dtype),
            pltpu.VMEM((planes, width, depth), jnp.float32),
            pltpu.SemaphoreType.DMA((1,)),
        ],
        "pack_own",
    )
    window = (comps, planes, cols + 2, snaps, depth)
    outs = call(
        functools.partial(pack_away_kernel, chips, planes, cols),
        [(comps, 2 * planes, snaps, depth)] + [window] * (2 * chips - 1),
        own[0],
        [],
        "pack_away",
    )
    return own, outs[0], outs[1], outs[2 : chips + 1], outs[chips + 1 :]


def fetch_all(views, slots, sem):
    copies = [pltpu.make_async_copy(view, slot, sem) for view, slot in zip(views, slots)]
    for item in copies:
        item.start()
    for item in copies:
        item.wait()


def coefficients(own, low, high, metric, large, coef, first):
    comps, (_, planes, cols, depth) = 3, metric.shape
    width = large.shape[2]

    def rolled(comp, plane):
        if plane < 0 or plane == planes:
            near = low if plane < 0 else high
            rows = [near[comp, piece] for piece in range(cols, near.shape[1])]
            return jnp.concatenate(rows, axis=0).astype(jnp.float32)[:cols]
        values = large[comp, plane].astype(jnp.float32)
        return pltpu.roll(values, lax.rem(width + 1 - first, width), 0)

    def at(comp, plane):
        values = rolled(comp, plane)
        return values if plane in (-1, planes) else values[1 : cols + 1]

    for plane in range(planes):
        half_x, half_shear, half_y, half_z = [0.5 * metric[k, plane] for k in range(4)]
        step_y = [at(comp, plane + 1) - at(comp, plane - 1) for comp in range(comps)]
        step_z = [along_z(at(comp, plane)) for comp in range(2)]
        after = [rolled(comp, plane)[2 : cols + 2] for comp in (1, 2)]
        before = [rolled(comp, plane)[:cols] for comp in (1, 2)]
        rows = [
            half_x,
            half_shear,
            half_y,
            half_z,
            half_y * step_y[2] - half_z * step_z[1],
            half_z * step_z[0] - half_shear * step_y[2],
            half_shear * step_y[1] - half_y * step_y[0],
            half_x * after[0],
            half_x * before[0],
            half_x * after[1],
            half_x * before[1],
        ]
        for index, value in enumerate(rows):
            coef[plane, index] = value


def along_z(values):
    depth = values.shape[-1]
    return pltpu.roll(values, depth - 1, 1) - pltpu.roll(values, 1, 1)


def curl(get, row, mods, plane, col):
    def value(comp, plane_at, col_at):
        return get(comp, plane_at, col_at).astype(jnp.float32)

    gx, shear, gy, gz, ax, ay, az, v_after, v_before, w_after, w_before = row
    mod_before, mod_here, mod_after = mods
    dy_u, dy_v, dy_w = [value(k, plane + 1, col) - value(k, plane - 1, col) for k in range(3)]
    dz_u, dz_v = [along_z(value(k, plane, col)) for k in range(2)]
    dx_v, dx_w = [value(k, plane, col + 1) - value(k, plane, col - 1) for k in (1, 2)]
    around_x = gy * dy_w - gz * dz_v + mod_here * ax
    around_y = (
        gz * dz_u - gx * dx_w - shear * dy_w + mod_here * ay
        - (mod_after * w_after - mod_before * w_before)
    )
    around_z = (
        gx * dx_v + shear * dy_v - gy * dy_u + mod_here * az
        + (mod_after * v_after - mod_before * v_before)
    )
    return around_x, around_y, around_z


def split(value):
    top = value.astype(jnp.bfloat16)
    return top, (value - top.astype(jnp.float32)).astype(jnp.bfloat16)


def rows_of(chips, step, part, snaps):
    chip, core = whereabouts()
    owner = lax.rem(chip + chips - step, chips) * CORES + (1 - core if part else core)
    return pl.multiple_of(owner * snaps, snaps)


def curls(chips, gets, steps, coef, amplitude, plane, cols, snaps, store):
    depth = amplitude.shape[2]
    for col in range(cols):
        row = [
            jnp.broadcast_to(coef[plane, index, pl.ds(col, 1), :], (snaps, depth))
            for index in range(11)
        ]
        for step in steps:
            for part in range(CORES):
                start = rows_of(chips, step, part, snaps)
                mods = [amplitude[col + k, pl.ds(start, snaps), :] for k in range(3)]
                get = functools.partial(gets, step, part)
                for comp, value in enumerate(curl(get, row, mods, plane, col)):
                    store(comp, col, step, part, start, split(value))


def near_kernel(chips, planes, modulation, metric, large, *refs):
    sources, refs = refs[: planes + 6], refs[planes + 6 :]
    early, coef, amplitude = refs[:3]
    slots, sem = refs[3:-1], refs[-1]
    snaps = early.shape[5]
    cols = early.shape[2]
    chip, core = whereabouts()
    first = pl.multiple_of((chip * CORES + core) * cols, 8)
    views = [modulation, metric.at[:, :, pl.ds(first, cols)], large]
    views += [item.at[:, core] for item in sources[:planes]]
    edge, other, low, high, low_other, high_other = sources[planes:]
    views += [edge, other, low.at[:, core], high.at[:, core], low_other, high_other]
    fetch_all(views, slots, sem.at[0])
    mod, metric, large = slots[:3]
    own = slots[3 : planes + 3]
    edge, other, low, high, low_other, high_other = slots[planes + 3 :]

    wide = jnp.concatenate([mod[...], mod[...]], axis=1)
    wide = pltpu.roll(wide, lax.rem(wide.shape[1] + 1 - first, wide.shape[1]), 1)
    for col in range(cols + 2):
        amplitude[col] = jnp.broadcast_to(wide[:, col : col + 1], amplitude.shape[1:])
    coefficients(own, low, high, metric, large, coef, first)

    def gets(step, part, comp, plane, col):
        if plane < 0:
            return (low_other if part else low)[comp, col]
        if plane == planes:
            return (high_other if part else high)[comp, col]
        if part:
            return other[comp, plane, col + 1]
        if col in (-1, cols):
            return edge[comp, 2 * plane + (col > 0)]
        return own[plane][comp, col]

    for plane in range(planes):

        def store(comp, col, step, part, start, halves):
            for level in range(2):
                early[comp, plane, col, level, part] = halves[level]

        curls(chips, gets, [0], coef, amplitude, plane, cols, snaps, store)


def near_stage(modulation, metric, large, sources, chips, cols):
    everyone, width = modulation.shape
    comps, planes, _, depth = large.shape
    snaps = everyone // (chips * CORES)
    whole = pl.BlockSpec(memory_space=pltpu.VMEM)
    shapes = [item.shape for item in sources]
    halved = [shape[:1] + shape[2:] for shape in shapes]
    shapes = halved[:planes] + shapes[planes : planes + 2] + halved[planes + 2 : planes + 4] + shapes[planes + 4 :]
    slots = [
        pltpu.VMEM(modulation.shape, modulation.dtype),
        pltpu.VMEM((4, planes, cols, depth), metric.dtype),
        pltpu.VMEM(large.shape, large.dtype),
    ]
    slots += [pltpu.VMEM(shape, large.dtype) for shape in shapes]
    return pl.pallas_call(
        functools.partial(near_kernel, chips, planes),
        in_specs=[pl.BlockSpec(memory_space=pl.ANY)] * (3 + len(sources)),
        out_specs=[whole] * 3,
        out_shape=[
            jax.ShapeDtypeStruct((comps, planes, cols, 2, CORES, snaps, depth), jnp.bfloat16),
            jax.ShapeDtypeStruct((planes, 11, cols, depth), jnp.float32),
            jax.ShapeDtypeStruct((cols + 2, everyone, depth), jnp.float32),
        ],
        scratch_shapes=slots + [pltpu.SemaphoreType.DMA((1,))],
        compiler_params=pltpu.CompilerParams(vmem_limit_bytes=VMEM_BYTES),
        cost_estimate=pl.CostEstimate(flops=0, bytes_accessed=8 << 20, transcendentals=0),
        name="near_stage",
    )(modulation, metric, large, *sources)


def far_kernel(chips, keys, first, planes, coef, amplitude, early, before, *refs):
    sources, refs = refs[: len(keys)], refs[len(keys) :]
    parts, gram, total = refs[:3]
    slots, sem = refs[3:-1], refs[-1]
    arrays = dict(zip(keys, slots))
    cols = early.shape[2]
    snaps = early.shape[5]
    everyone = amplitude.shape[1]
    fetch_all(sources, slots, sem.at[0])

    def gets(step, part, comp, plane, col):
        span = slice(part * snaps, (part + 1) * snaps)
        if 0 <= plane < planes and col in (-1, cols):
            return arrays[step, "edge"][comp, 2 * plane + (col > 0), span]
        name = "low" if plane < 0 else "high" if plane == planes else plane
        return arrays[step, name][comp, col, span]

    total[...] = jnp.zeros_like(total)
    for index in range(parts.shape[1]):
        plane = first + index

        def store(comp, col, step, part, start, halves):
            for level in range(2):
                parts[comp, index, col, pl.ds(start + level * everyone, snaps), :] = halves[level]

        for part in range(CORES):
            start = rows_of(chips, 0, part, snaps)
            for comp in range(3):
                for col in range(cols):
                    halves = [early[comp, plane, col, level, part] for level in range(2)]
                    store(comp, col, 0, part, start, halves)
        steps = range(1, chips)
        curls(chips, gets, steps, coef, amplitude, plane, cols, snaps, store)
        for comp in range(3):
            for col in range(0, cols, 2):
                both = jnp.concatenate([parts[comp, index, col], parts[comp, index, col + 1]], 1)
                total[...] += lax.dot_general(
                    both, both, (((1,), (1,)), ((), ())), preferred_element_type=jnp.float32
                )
    gram[...] = before[...] + (
        total[:everyone, :everyone]
        + total[everyone:, everyone:]
        + (total[:everyone, everyone:] + total[everyone:, :everyone])
    )


def far_stage(coef, amplitude, early, before, arrays, chips, first, last):
    comps, planes, cols, _, _, snaps, depth = early.shape
    everyone = snaps * chips * CORES
    wanted = {"edge"} | set(range(max(first - 1, 0), min(last + 1, planes)))
    if first == 0:
        wanted.add("low")
    if last == planes:
        wanted.add("high")
    chosen = {key: item for key, item in arrays.items() if key[1] in wanted}
    whole = pl.BlockSpec(memory_space=pltpu.VMEM)
    return pl.pallas_call(
        functools.partial(far_kernel, chips, tuple(chosen), first, planes),
        in_specs=[whole] * 4 + [pl.BlockSpec(memory_space=pl.ANY)] * len(chosen),
        out_specs=[whole, whole],
        out_shape=[
            jax.ShapeDtypeStruct((comps, last - first, cols, 2 * everyone, depth), jnp.bfloat16),
            jax.ShapeDtypeStruct((everyone, everyone), jnp.float32),
        ],
        scratch_shapes=[pltpu.VMEM((2 * everyone, 2 * everyone), jnp.float32)]
        + [pltpu.VMEM(item.shape, item.dtype) for item in chosen.values()]
        + [pltpu.SemaphoreType.DMA((1,))],
        compiler_params=pltpu.CompilerParams(vmem_limit_bytes=VMEM_BYTES),
        cost_estimate=pl.CostEstimate(flops=0, bytes_accessed=8 << 20, transcendentals=0),
        name="far_stage",
    )(coef, amplitude, early, before, *chosen.values())


def whiten_kernel(count, gram, *refs):
    pieces, (out, slots, sems) = refs[:-3], refs[-3:]
    everyone = gram.shape[0]
    comps, cols, depth = pieces[0].shape[0], pieces[0].shape[2], pieces[0].shape[4]
    pitch = slots.shape[1] // everyone

    def dot(a, b):
        return jnp.dot(a, b, precision=lax.Precision.HIGHEST, preferred_element_type=jnp.float32)

    correlation = gram[...] / count
    frob_scale = jnp.sqrt(jnp.sum(correlation * correlation, keepdims=True) + 1e-06)
    approx = correlation / frob_scale
    row = lax.broadcasted_iota(jnp.int32, (everyone, everyone), 0)
    col = lax.broadcasted_iota(jnp.int32, (everyone, everyone), 1)
    diagonal = jnp.where(row == col, 3.0, 0.0)
    factor = 0.5 * (diagonal - approx)
    inverse = factor
    for _ in range(1, NSITER):
        approx = dot(approx, factor)
        factor = 0.5 * (diagonal - dot(inverse, approx))
        inverse = dot(factor, inverse)
    top, rest = split(inverse / jnp.sqrt(frob_scale))
    left = jnp.concatenate([top, top, rest, rest], axis=1)
    slot, plane, copies = 0, 0, []
    for piece in pieces:
        for index in range(piece.shape[1]):
            for comp in range(comps):
                for first in range(0, cols, 2):
                    both = [piece[comp, index, first], piece[comp, index, first + 1]]
                    both = jnp.concatenate(both, axis=1)
                    mixed = jnp.dot(
                        left,
                        jnp.concatenate([both, both], axis=0),
                        preferred_element_type=jnp.float32,
                    )
                    for sub in range(2):
                        slots[slot, pl.ds(first + sub, everyone, stride=pitch), :] = mixed[
                            :, sub * depth : (sub + 1) * depth
                        ]
                source = slots.reshape(slots.shape[0], everyone, pitch, depth)
                copies.append(
                    pltpu.make_async_copy(
                        source.at[slot, :, pl.ds(0, cols)],
                        out.at[:, comp, plane],
                        sems.at[slot],
                    )
                )
                copies[-1].start()
                slot += 1
            plane += 1
    for item in copies:
        item.wait()


def whiten(gram, pieces, count):
    everyone = gram.shape[0]
    comps, _, cols, _, depth = pieces[0].shape
    planes = sum(piece.shape[1] for piece in pieces)
    pitch = cols + 8 if (cols // 8) % 2 == 0 else cols
    whole = pl.BlockSpec(memory_space=pltpu.VMEM)
    return pl.pallas_call(
        functools.partial(whiten_kernel, count),
        in_specs=[whole] * (1 + len(pieces)),
        out_specs=pl.BlockSpec(memory_space=pl.ANY),
        out_shape=jax.ShapeDtypeStruct((everyone, comps, planes, cols, depth), jnp.float32),
        scratch_shapes=[
            pltpu.VMEM((comps * planes, everyone * pitch, depth), jnp.float32),
            pltpu.SemaphoreType.DMA((comps * planes,)),
        ],
        compiler_params=pltpu.CompilerParams(vmem_limit_bytes=VMEM_BYTES),
        name="whiten",
    )(gram, *pieces)


def to_chip(array, step):
    count = lax.axis_size("snap")
    pairs = [(i, (i + step * CORES) % count) for i in range(count)]
    return lax.ppermute(array, "snap", pairs)


def to_core(array):
    return lax.ppermute(array, "snap", [(i, i ^ 1) for i in range(lax.axis_size("snap"))])


def to_slab(array, step):
    count = lax.axis_size("slab")
    pairs = [(i, i + step) for i in range(count) if 0 <= i + step < count]
    return lax.ppermute(array, "slab", pairs)


def all_sum(value):
    for axis in ("snap", "slab"):
        count = lax.axis_size(axis)
        if count & (count - 1):
            value = lax.psum(value, axis)
            continue
        stride = 1
        while stride < count:
            pairs = [(i, i ^ stride) for i in range(count)]
            value = value + lax.ppermute(value, axis, pairs)
            stride *= 2
    return value


def per_device(flow, large_scale, modulation, metric):
    snap_count = lax.axis_size("snap")
    slab_count = lax.axis_size("slab")
    _, comps, planes, width, depth = flow.shape
    chips = snap_count // CORES
    cols = width // snap_count
    core = lax.rem(lax.axis_index("snap"), CORES)

    def half(array):
        return lax.dynamic_index_in_dim(array, 1 - core, 1, keepdims=False)

    own, own_edge, own_other, mine, other = pack(flow, large_scale, chips, cols)
    low, high = to_slab(own[-1], 1), to_slab(own[0], -1)
    arrays = {}
    for step in range(1, chips):
        both = jnp.concatenate([mine[step - 1], to_core(other[step - 1])], axis=3)
        order = [planes - 1] + list(range(planes - 1))
        for plane in order:
            arrays[step, plane] = to_chip(both[:, plane, 1:-1], step)
        edge = jnp.stack([both[:, :, 0], both[:, :, -1]], axis=2)
        edge = edge.reshape(comps, 2 * planes, *edge.shape[3:])
        edge, _ = lax.optimization_barrier((edge, arrays[step, 0]))
        arrays[step, "edge"] = to_chip(edge, step)
        arrays[step, "low"] = to_slab(arrays[step, planes - 1], 1)
        arrays[step, "high"] = to_slab(arrays[step, 0], -1)
    sources = own + [own_edge, to_core(own_other), low, high]
    sources += [to_core(half(low)), to_core(half(high))]
    early, coef, amplitude = near_stage(modulation, metric, large_scale, sources, chips, cols)
    gram = jnp.zeros(modulation.shape[:1] * 2, jnp.float32)
    pieces = []
    for begin, end in ((0, planes - 1), (planes - 1, planes)):
        if begin < end:
            piece, gram = far_stage(coef, amplitude, early, gram, arrays, chips, begin, end)
            pieces.append(piece)
    return whiten(all_sum(gram), pieces, float(comps * planes * slab_count * width * depth))


def solution(mesh):
    return jax.shard_map(
        per_device,
        mesh=mesh,
        in_specs=(
            P("snap", None, "slab", None, None),
            P(None, "slab", None, None),
            P(),
            P(None, "slab", None, None),
        ),
        out_specs=P(None, None, "slab", "snap", None),
        check_vma=False,
    )
```

```python
import functools

import jax
import jax.numpy as jnp
from jax import lax
from jax.experimental import pallas as pl
from jax.experimental.pallas import tpu as pltpu
from jax.sharding import PartitionSpec as P

NSITER = 6
CORES = 2
VMEM_BYTES = 16 * 1024 * 1024


def whereabouts():
    place = lax.axis_index("snap")
    return lax.div(place, CORES), lax.rem(place, CORES)


def plane_at(slot, planes):
    upper = lax.rem(lax.axis_index("slab"), 2)
    if slot == 0:
        return (1 - upper) * (planes - 1)
    if slot == 1:
        return upper * (planes - 1)
    return slot - 1


def halo_at(slot, planes):
    upper = lax.rem(lax.axis_index("slab"), 2)
    return (1 - upper if slot == 0 else upper) * (planes + 1)


def pack_columns(flow, flat, plane):
    snaps, width = flow.shape[0], flow.shape[3]
    pitch = width + 1
    for snap in range(snaps):
        flat[pl.ds(snap * pitch, width), :] = flow[snap, 0, plane].astype(jnp.float32)

    def column(col):
        return flat[pl.ds(col, snaps, stride=pitch), :].astype(jnp.bfloat16)

    return column


def pack_own_kernel(planes, cols, flow, large, *refs):
    own, (flat, near, large_rows, sem) = refs[:-4], refs[-4:]
    snaps = flow.shape[0]
    extra = own[0].shape[2] - cols
    chip, _ = whereabouts()
    comp = pl.program_id(0)
    fetch = pltpu.make_async_copy(large.at[comp], near, sem.at[0])
    fetch.start()
    for slot in range(planes):
        column = pack_columns(flow, flat, plane_at(slot, planes))
        for part in range(CORES):
            start = chip * (CORES * cols) + part * cols
            for col in range(cols):
                own[slot][0, part, col] = column(start + col)
    fetch.wait()
    large_rows[...] = near[...].astype(jnp.float32)
    for slot in range(planes):
        for part in range(CORES):
            start = chip * (CORES * cols) + part * cols
            rows = large_rows[plane_at(slot, planes), pl.ds(pl.multiple_of(start, 8), cols), :]
            if cols < extra * snaps:
                rows = jnp.concatenate([rows] * (extra * snaps // cols), axis=0)
            for piece in range(extra):
                tile = rows[piece * snaps : (piece + 1) * snaps]
                own[slot][0, part, cols + piece] = tile.astype(jnp.bfloat16)


def pack_windows_kernel(chips, planes, cols, mine, flow, first, *refs):
    outs, flat = refs[:-1], refs[-1]
    width = flow.shape[3]
    chip, core = whereabouts()
    part = core if mine else 1 - core
    for slot in range(planes):
        column = pack_columns(flow, flat, plane_at(slot, planes))
        for target, step in zip(outs, [*range(1, chips), 0]):
            start = lax.rem(chip + step, chips) * (CORES * cols) + part * cols
            left = column(lax.rem(start - 1 + width, width))
            right = column(lax.rem(start + cols, width))
            if mine and step == 0:
                target[0, 2 * slot] = left
                target[0, 2 * slot + 1] = right
                continue
            target[0, slot, 0] = left
            for col in range(cols):
                target[0, slot, col + 1] = column(start + col)
            target[0, slot, cols + 1] = right


def pack(flow, large, chips, cols):
    snaps, comps, planes, width, depth = flow.shape
    extra = -(-cols // snaps)

    def spec(shape):
        tail = len(shape) - 1
        return pl.BlockSpec((1,) + shape[1:], lambda comp: (comp,) + (0,) * tail)

    def call(kernel, shapes, second, scratch, name):
        return list(
            pl.pallas_call(
                kernel,
                grid=(comps,),
                in_specs=[
                    pl.BlockSpec((snaps, 1, planes, width, depth), lambda comp: (0, comp, 0, 0, 0)),
                    pl.BlockSpec(memory_space=pl.ANY),
                ],
                out_specs=[spec(shape) for shape in shapes],
                out_shape=[jax.ShapeDtypeStruct(shape, flow.dtype) for shape in shapes],
                scratch_shapes=[pltpu.VMEM((snaps * (width + 1), depth), jnp.float32)] + scratch,
                compiler_params=pltpu.CompilerParams(vmem_limit_bytes=VMEM_BYTES),
                name=name,
            )(flow, second)
        )

    own = call(
        functools.partial(pack_own_kernel, planes, cols),
        [(comps, CORES, cols + extra, snaps, depth)] * planes,
        large,
        [
            pltpu.VMEM((planes, width, depth), large.dtype),
            pltpu.VMEM((planes, width, depth), jnp.float32),
            pltpu.SemaphoreType.DMA((1,)),
        ],
        "pack_own",
    )
    window = (comps, planes, cols + 2, snaps, depth)
    edge = (comps, 2 * planes, snaps, depth)
    other = call(
        functools.partial(pack_windows_kernel, chips, planes, cols, False),
        [window] * chips,
        own[0],
        [],
        "pack_other",
    )
    mine = call(
        functools.partial(pack_windows_kernel, chips, planes, cols, True),
        [window] * (chips - 1) + [edge],
        other[0],
        [],
        "pack_mine",
    )
    return own, mine, other


def coefficients(wide, metric, large, coef, first):
    comps, (_, planes, cols, depth) = 3, metric.shape
    width = large.shape[2]

    def rolled(comp, plane):
        values = large[comp, plane].astype(jnp.float32)
        return pltpu.roll(values, lax.rem(width + 1 - first, width), 0)

    def at(comp, plane):
        if 0 <= plane < planes:
            return rolled(comp, plane)[1 : cols + 1]
        side = 0 if plane < 0 else 1
        rows = [wide[side, comp, piece] for piece in range(wide.shape[2])]
        return jnp.concatenate(rows, axis=0).astype(jnp.float32)[:cols]

    for plane in range(planes):
        half_x, half_shear, half_y, half_z = [0.5 * metric[k, plane] for k in range(4)]
        step_y = [at(comp, plane + 1) - at(comp, plane - 1) for comp in range(comps)]
        step_z = [along_z(at(comp, plane)) for comp in range(2)]
        after = [rolled(comp, plane)[2 : cols + 2] for comp in (1, 2)]
        before = [rolled(comp, plane)[:cols] for comp in (1, 2)]
        rows = [
            half_x,
            half_shear,
            half_y,
            half_z,
            half_y * step_y[2] - half_z * step_z[1],
            half_z * step_z[0] - half_shear * step_y[2],
            half_shear * step_y[1] - half_y * step_y[0],
            half_x * after[0],
            half_x * before[0],
            half_x * after[1],
            half_x * before[1],
        ]
        for index, value in enumerate(rows):
            coef[plane, index] = value


def along_z(values):
    depth = values.shape[-1]
    return pltpu.roll(values, depth - 1, 1) - pltpu.roll(values, 1, 1)


def curl(get, row, mods, plane, col):
    def value(comp, plane_at, col_at):
        return get(comp, plane_at, col_at).astype(jnp.float32)

    gx, shear, gy, gz, ax, ay, az, v_after, v_before, w_after, w_before = row
    mod_before, mod_here, mod_after = mods
    dy_u, dy_v, dy_w = [value(k, plane + 1, col) - value(k, plane - 1, col) for k in range(3)]
    dz_u, dz_v = [along_z(value(k, plane, col)) for k in range(2)]
    dx_v, dx_w = [value(k, plane, col + 1) - value(k, plane, col - 1) for k in (1, 2)]
    around_x = gy * dy_w - gz * dz_v + mod_here * ax
    around_y = (
        gz * dz_u - gx * dx_w - shear * dy_w + mod_here * ay
        - (mod_after * w_after - mod_before * w_before)
    )
    around_z = (
        gx * dx_v + shear * dy_v - gy * dy_u + mod_here * az
        + (mod_after * v_after - mod_before * v_before)
    )
    return around_x, around_y, around_z


def split(value):
    top = value.astype(jnp.bfloat16)
    return top, (value - top.astype(jnp.float32)).astype(jnp.bfloat16)


def rows_of(chips, step, part, snaps):
    chip, core = whereabouts()
    owner = lax.rem(chip + chips - step, chips) * CORES + (1 - core if part else core)
    return pl.multiple_of(owner * snaps, snaps)


def curls(chips, field, steps, coef, amplitude, plane, cols, snaps, store):
    depth = amplitude.shape[2]
    for col in range(cols):
        row = [
            jnp.broadcast_to(coef[plane, index, pl.ds(col, 1), :], (snaps, depth))
            for index in range(11)
        ]
        for step in steps:
            for part in range(CORES):
                start = rows_of(chips, step, part, snaps)
                mods = [amplitude[col + k, pl.ds(start, snaps), :] for k in range(3)]
                get = functools.partial(field, step, part)
                for comp, value in enumerate(curl(get, row, mods, plane + 1, col + 1)):
                    store(comp, col, step, part, start, split(value))


def near_kernel(chips, planes, modulation, metric, large, *refs):
    own, (edge, other, pair, away, pair_other, away_other) = refs[:planes], refs[planes : planes + 6]
    early, coef, amplitude, mod, metric_mine, large_mine, wide, field, sem = refs[planes + 6 :]
    snaps, cols = early.shape[5], early.shape[2]
    extra = wide.shape[2]
    chip, core = whereabouts()
    first = pl.multiple_of((chip * CORES + core) * cols, 8)
    middle, left, right = pl.ds(1, cols), pl.ds(0, 1), pl.ds(cols + 1, 1)
    moves = [
        (modulation, mod),
        (metric.at[:, :, pl.ds(first, cols)], metric_mine),
        (large, large_mine),
    ]
    for slot in range(planes):
        plane = plane_at(slot, planes) + 1
        moves += [
            (own[slot].at[:, core, pl.ds(0, cols)], field.at[0, plane, :, middle]),
            (edge.at[:, pl.ds(2 * slot, 1)], field.at[0, plane, :, left]),
            (edge.at[:, pl.ds(2 * slot + 1, 1)], field.at[0, plane, :, right]),
            (other.at[:, slot], field.at[1, plane]),
        ]
    for slot, (close, far) in enumerate(((pair, pair_other), (away, away_other))):
        halo = halo_at(slot, planes)
        moves += [
            (close.at[:, core, pl.ds(0, cols)], field.at[0, halo, :, middle]),
            (far.at[:, pl.ds(0, cols)], field.at[1, halo, :, middle]),
            (close.at[:, core, pl.ds(cols, extra)], wide.at[jnp.minimum(halo, 1)]),
        ]
    fetch_all(moves, sem.at[0])

    doubled = jnp.concatenate([mod[...], mod[...]], axis=1)
    doubled = pltpu.roll(doubled, lax.rem(doubled.shape[1] + 1 - first, doubled.shape[1]), 1)
    for col in range(cols + 2):
        amplitude[col] = jnp.broadcast_to(doubled[:, col : col + 1], amplitude.shape[1:])
    coefficients(wide, metric_mine, large_mine, coef, first)

    def tile(step, part, comp, plane, col):
        return field[part, plane, comp, col]

    for slot in range(planes):

        def store(comp, col, step, part, start, halves):
            for level in range(2):
                early[comp, slot, col, level, part] = halves[level]

        curls(chips, tile, [0], coef, amplitude, plane_at(slot, planes), cols, snaps, store)


def fetch_all(moves, sem):
    copies = [pltpu.make_async_copy(source, target, sem) for source, target in moves]
    for item in copies:
        item.start()
    for item in copies:
        item.wait()


def near_stage(modulation, metric, large, sources, chips, cols):
    everyone, _ = modulation.shape
    comps, planes, _, depth = large.shape
    snaps = everyone // (chips * CORES)
    extra = sources[0].shape[2] - cols
    whole = pl.BlockSpec(memory_space=pltpu.VMEM)
    return pl.pallas_call(
        functools.partial(near_kernel, chips, planes),
        in_specs=[pl.BlockSpec(memory_space=pl.ANY)] * (3 + len(sources)),
        out_specs=[whole] * 3,
        out_shape=[
            jax.ShapeDtypeStruct((comps, planes, cols, 2, CORES, snaps, depth), jnp.bfloat16),
            jax.ShapeDtypeStruct((planes, 11, cols, depth), jnp.float32),
            jax.ShapeDtypeStruct((cols + 2, everyone, depth), jnp.float32),
        ],
        scratch_shapes=[
            pltpu.VMEM(modulation.shape, modulation.dtype),
            pltpu.VMEM((4, planes, cols, depth), metric.dtype),
            pltpu.VMEM(large.shape, large.dtype),
            pltpu.VMEM((2, comps, extra, snaps, depth), large.dtype),
            pltpu.VMEM((CORES, planes + 2, comps, cols + 2, snaps, depth), large.dtype),
            pltpu.SemaphoreType.DMA((1,)),
        ],
        compiler_params=pltpu.CompilerParams(vmem_limit_bytes=VMEM_BYTES),
        cost_estimate=pl.CostEstimate(flops=0, bytes_accessed=8 << 20, transcendentals=0),
        name="near_stage",
    )(modulation, metric, large, *sources)


def far_kernel(chips, planes, slots, halo, coef, amplitude, early, before, *refs):
    sources, (parts, gram, field, total, sem) = list(refs[:-5]), refs[-5:]
    cols, snaps = early.shape[2], early.shape[5]
    everyone = amplitude.shape[1]
    middle, left, right = pl.ds(1, cols), pl.ds(0, 1), pl.ds(cols + 1, 1)
    moves = []
    for step in range(1, chips):
        own = [sources.pop(0) for _ in range(planes)]
        edge, beyond = sources.pop(0), sources.pop(0)
        for slot in range(planes):
            target = field.at[step - 1, plane_at(slot, planes) + 1]
            moves += [
                (own[slot], target.at[:, middle]),
                (edge.at[:, pl.ds(2 * slot, 1)], target.at[:, left]),
                (edge.at[:, pl.ds(2 * slot + 1, 1)], target.at[:, right]),
            ]
        moves.append((beyond, field.at[step - 1, halo_at(halo, planes), :, middle]))
    fetch_all(moves, sem.at[0])

    def tile(step, part, comp, plane, col):
        return field[step - 1, plane, comp, col, part * snaps : (part + 1) * snaps]

    total[...] = jnp.zeros_like(total)
    for index, slot in enumerate(slots):

        def store(comp, col, step, part, start, halves):
            for level in range(2):
                parts[comp, index, col, pl.ds(start + level * everyone, snaps), :] = halves[level]

        for part in range(CORES):
            start = rows_of(chips, 0, part, snaps)
            for comp in range(3):
                for col in range(cols):
                    halves = [early[comp, slot, col, level, part] for level in range(2)]
                    store(comp, col, 0, part, start, halves)
        steps = range(1, chips)
        plane = plane_at(slot, planes)
        curls(chips, tile, steps, coef, amplitude, plane, cols, snaps, store)
        for comp in range(3):
            for col in range(0, cols, 2):
                both = jnp.concatenate([parts[comp, index, col], parts[comp, index, col + 1]], 1)
                total[...] += lax.dot_general(
                    both, both, (((1,), (1,)), ((), ())), preferred_element_type=jnp.float32
                )
    gram[...] = before[...] + (
        total[:everyone, :everyone]
        + total[everyone:, everyone:]
        + (total[:everyone, everyone:] + total[everyone:, :everyone])
    )


def far_stage(coef, amplitude, early, before, sources, chips, slots, halo):
    comps, planes, cols, _, _, snaps, depth = early.shape
    everyone = snaps * chips * CORES
    whole = pl.BlockSpec(memory_space=pltpu.VMEM)
    return pl.pallas_call(
        functools.partial(far_kernel, chips, planes, slots, halo),
        in_specs=[whole] * 4 + [pl.BlockSpec(memory_space=pl.ANY)] * len(sources),
        out_specs=[whole, whole],
        out_shape=[
            jax.ShapeDtypeStruct((comps, len(slots), cols, 2 * everyone, depth), jnp.bfloat16),
            jax.ShapeDtypeStruct((everyone, everyone), jnp.float32),
        ],
        scratch_shapes=[
            pltpu.VMEM(
                (chips - 1, planes + 2, comps, cols + 2, CORES * snaps, depth), jnp.bfloat16
            ),
            pltpu.VMEM((2 * everyone, 2 * everyone), jnp.float32),
            pltpu.SemaphoreType.DMA((1,)),
        ],
        compiler_params=pltpu.CompilerParams(vmem_limit_bytes=VMEM_BYTES),
        cost_estimate=pl.CostEstimate(flops=0, bytes_accessed=8 << 20, transcendentals=0),
        name="far_stage",
    )(coef, amplitude, early, before, *sources)


def whiten_kernel(count, gram, *refs):
    pieces, (out, slots, sems) = refs[:-3], refs[-3:]
    everyone = gram.shape[0]
    comps, cols, depth = pieces[0].shape[0], pieces[0].shape[2], pieces[0].shape[4]
    pitch = slots.shape[1] // everyone

    def dot(a, b):
        return jnp.dot(a, b, precision=lax.Precision.HIGHEST, preferred_element_type=jnp.float32)

    correlation = gram[...] / count
    frob_scale = jnp.sqrt(jnp.sum(correlation * correlation, keepdims=True) + 1e-06)
    approx = correlation / frob_scale
    row = lax.broadcasted_iota(jnp.int32, (everyone, everyone), 0)
    col = lax.broadcasted_iota(jnp.int32, (everyone, everyone), 1)
    diagonal = jnp.where(row == col, 3.0, 0.0)
    factor = 0.5 * (diagonal - approx)
    inverse = factor
    for _ in range(1, NSITER):
        approx = dot(approx, factor)
        factor = 0.5 * (diagonal - dot(inverse, approx))
        inverse = dot(factor, inverse)
    top, rest = split(inverse / jnp.sqrt(frob_scale))
    left = jnp.concatenate([top, top, rest, rest], axis=1)
    slot, copies = 0, []
    planes = sum(piece.shape[1] for piece in pieces)
    order = [1] + list(range(2, planes)) + [0]
    for piece in pieces:
        for index in range(piece.shape[1]):
            plane = plane_at(order.pop(0), planes)
            for comp in range(comps):
                for first in range(0, cols, 2):
                    both = [piece[comp, index, first], piece[comp, index, first + 1]]
                    both = jnp.concatenate(both, axis=1)
                    mixed = jnp.dot(
                        left,
                        jnp.concatenate([both, both], axis=0),
                        preferred_element_type=jnp.float32,
                    )
                    for sub in range(2):
                        slots[slot, pl.ds(first + sub, everyone, stride=pitch), :] = mixed[
                            :, sub * depth : (sub + 1) * depth
                        ]
                source = slots.reshape(slots.shape[0], everyone, pitch, depth)
                copies.append(
                    pltpu.make_async_copy(
                        source.at[slot, :, pl.ds(0, cols)],
                        out.at[:, comp, plane],
                        sems.at[slot],
                    )
                )
                copies[-1].start()
                slot += 1
    for item in copies:
        item.wait()


def whiten(gram, pieces, count):
    everyone = gram.shape[0]
    comps, _, cols, _, depth = pieces[0].shape
    planes = sum(piece.shape[1] for piece in pieces)
    pitch = cols + 8 if (cols // 8) % 2 == 0 else cols
    whole = pl.BlockSpec(memory_space=pltpu.VMEM)
    return pl.pallas_call(
        functools.partial(whiten_kernel, count),
        in_specs=[whole] * (1 + len(pieces)),
        out_specs=pl.BlockSpec(memory_space=pl.ANY),
        out_shape=jax.ShapeDtypeStruct((everyone, comps, planes, cols, depth), jnp.float32),
        scratch_shapes=[
            pltpu.VMEM((comps * planes, everyone * pitch, depth), jnp.float32),
            pltpu.SemaphoreType.DMA((comps * planes,)),
        ],
        compiler_params=pltpu.CompilerParams(vmem_limit_bytes=VMEM_BYTES),
        name="whiten",
    )(gram, *pieces)


def to_chip(array, step):
    count = lax.axis_size("snap")
    pairs = [(i, (i + step * CORES) % count) for i in range(count)]
    return lax.ppermute(array, "snap", pairs)


def to_core(array):
    return lax.ppermute(array, "snap", [(i, i ^ 1) for i in range(lax.axis_size("snap"))])


def to_pair(array, first):
    count = lax.axis_size("slab")
    pairs = [(i, i + 1) for i in range(first, count - 1, 2)]
    return lax.ppermute(array, "slab", pairs + [(j, i) for i, j in pairs])


def all_sum(value):
    for axis in ("snap", "slab"):
        count = lax.axis_size(axis)
        if count & (count - 1):
            value = lax.psum(value, axis)
            continue
        stride = 1
        while stride < count:
            pairs = [(i, i ^ stride) for i in range(count)]
            value = value + lax.ppermute(value, axis, pairs)
            stride *= 2
    return value


def per_device(flow, large_scale, modulation, metric):
    snap_count = lax.axis_size("snap")
    slab_count = lax.axis_size("slab")
    _, comps, planes, width, depth = flow.shape
    chips = snap_count // CORES
    cols = width // snap_count
    core = lax.rem(lax.axis_index("snap"), CORES)

    def half(array):
        return lax.dynamic_index_in_dim(array, 1 - core, 1, keepdims=False)

    assert planes >= 2
    own, mine, other = pack(flow, large_scale, chips, cols)
    pair = to_pair(own[0], 0)
    outer, arrays = own[1], []
    for step in range(1, chips):
        both = jnp.concatenate([mine[step - 1], to_core(other[step - 1])], axis=3)
        outer, both = lax.optimization_barrier((outer, both))
        here = [to_chip(both[:, slot, 1:-1], step) for slot in range(planes)]
        edge = jnp.stack([both[:, :, 0], both[:, :, -1]], axis=2)
        edge = edge.reshape(comps, 2 * planes, *edge.shape[3:])
        edge, _ = lax.optimization_barrier((edge, here[0]))
        arrays.append((here + [to_chip(edge, step)], to_pair(here[0], 0), to_pair(here[1], 1)))
    away = to_pair(outer, 1)
    pair, away, _ = lax.optimization_barrier((pair, away, [here[:planes] for here, *_ in arrays]))
    sources = own + [mine[-1], to_core(other[-1]), pair, away]
    sources += [to_core(half(pair)), to_core(half(away))]
    early, coef, amplitude = near_stage(modulation, metric, large_scale, sources, chips, cols)
    gram = jnp.zeros(modulation.shape[:1] * 2, jnp.float32)
    pieces = []
    for slots, halo in (((1,) + tuple(range(2, planes)), 1), ((0,), 0)):
        sources = []
        for here, *halos in arrays:
            sources += here + [halos[halo]]
        piece, gram = far_stage(coef, amplitude, early, gram, sources, chips, slots, halo)
        pieces.append(piece)
    return whiten(all_sum(gram), pieces, float(comps * planes * slab_count * width * depth))


def solution(mesh):
    return jax.shard_map(
        per_device,
        mesh=mesh,
        in_specs=(
            P("snap", None, "slab", None, None),
            P(None, "slab", None, None),
            P(),
            P(None, "slab", None, None),
        ),
        out_specs=P(None, None, "slab", "snap", None),
        check_vma=False,
    )
```

```python
import functools

import jax
import jax.numpy as jnp
from jax import lax
from jax.experimental import pallas as pl
from jax.experimental.pallas import tpu as pltpu
from jax.sharding import PartitionSpec as P

NSITER = 6
CORES = 2
VMEM_BYTES = 16 * 1024 * 1024
PACK_BYTES = 58 * 1024 * 1024


def whereabouts():
    place = lax.axis_index("snap")
    return lax.div(place, CORES), lax.rem(place, CORES)


def plane_at(slot, planes):
    upper = lax.rem(lax.axis_index("slab"), 2)
    if slot == 0:
        return (1 - upper) * (planes - 1)
    if slot == 1:
        return upper * (planes - 1)
    return slot - 1


def halo_at(slot, planes):
    upper = lax.rem(lax.axis_index("slab"), 2)
    return (1 - upper if slot == 0 else upper) * (planes + 1)


def spread(flat, pitch, snaps, values_of):
    for snap in range(snaps):
        values = values_of(snap)
        flat[pl.ds(snap * pitch, values.shape[0]), :] = values.astype(jnp.float32)

    def column(col):
        return flat[pl.ds(col, snaps, stride=pitch), :].astype(jnp.bfloat16)

    return column


def pack_own_kernel(planes, cols, flow, large, *refs):
    own, (near, flat, near_large, rows, sems) = refs[:-5], refs[-5:]
    snaps, comps, span = flow.shape[0], flow.shape[1], CORES * cols
    chip, core = whereabouts()
    first = pl.multiple_of(chip * span, span)
    copies = {}
    for slot in range(planes):
        for comp in range(comps):
            index = slot * comps + comp
            copies[index] = pltpu.make_async_copy(
                flow.at[:, comp, plane_at(slot, planes), pl.ds(first, span)],
                near.at[index],
                sems.at[index],
            )
            copies[index].start()
    fetch = pltpu.make_async_copy(large, near_large, sems.at[planes * comps])
    fetch.start()
    for slot in range(planes):
        for comp in range(comps):
            index = slot * comps + comp
            copies[index].wait()
            column = spread(flat, span + 1, snaps, lambda snap: near[index, snap])
            for col in range(span):
                own[slot][comp, col] = column(col)
    fetch.wait()
    rows[...] = near_large[...].astype(jnp.float32)
    start = pl.multiple_of(first + core * cols, 8)
    for slot in range(planes):
        for comp in range(comps):
            values = rows[comp, plane_at(slot, planes), pl.ds(start, cols), :]
            if cols % snaps:
                values = jnp.concatenate([values] * (snaps // cols), axis=0)
            for piece in range(values.shape[0] // snaps):
                tile = values[piece * snaps : (piece + 1) * snaps]
                own[slot][comp, span + piece] = tile.astype(jnp.bfloat16)


def pack_windows_kernel(chips, planes, cols, kinds, flow, *refs):
    outs, flat = refs[:-1], refs[-1]
    snaps, width = flow.shape[0], flow.shape[3]
    chip, core = whereabouts()
    for slot in range(planes):
        plane = plane_at(slot, planes)
        column = spread(flat, width + 1, snaps, lambda snap: flow[snap, 0, plane])
        for target, (mine, step) in zip(outs, kinds):
            part = core if mine else 1 - core
            start = lax.rem(chip + step, chips) * (CORES * cols) + part * cols
            left = column(lax.rem(start - 1 + width, width))
            right = column(lax.rem(start + cols, width))
            if mine and step == 0:
                target[0, 2 * slot] = left
                target[0, 2 * slot + 1] = right
                continue
            target[0, slot, 0] = left
            for col in range(cols):
                target[0, slot, col + 1] = column(start + col)
            target[0, slot, cols + 1] = right


def pack(flow, large, chips, cols):
    snaps, comps, planes, width, depth = flow.shape
    extra, span = -(-cols // snaps), CORES * cols
    kind = flow.dtype
    params = pltpu.CompilerParams(vmem_limit_bytes=VMEM_BYTES)
    own = pl.pallas_call(
        functools.partial(pack_own_kernel, planes, cols),
        in_specs=[pl.BlockSpec(memory_space=pltpu.HBM)] * 2,
        out_specs=[pl.BlockSpec(memory_space=pltpu.VMEM)] * planes,
        out_shape=[jax.ShapeDtypeStruct((comps, span + extra, snaps, depth), kind)] * planes,
        scratch_shapes=[
            pltpu.VMEM((planes * comps, snaps, span, depth), kind),
            pltpu.VMEM((snaps * (span + 1), depth), jnp.float32),
            pltpu.VMEM(large.shape, kind),
            pltpu.VMEM(large.shape, jnp.float32),
            pltpu.SemaphoreType.DMA((planes * comps + 1,)),
        ],
        compiler_params=pltpu.CompilerParams(vmem_limit_bytes=PACK_BYTES),
        name="pack_own",
    )(flow, large)

    def windows(kinds, after, name):
        here, _ = lax.optimization_barrier((flow, after))

        def shape(mine, step):
            edge = mine and step == 0
            return (comps, 2 * planes) if edge else (comps, planes, cols + 2)

        shapes = [shape(*item) + (snaps, depth) for item in kinds]
        specs = [
            pl.BlockSpec((1,) + item[1:], lambda comp, tail=len(item) - 1: (comp,) + (0,) * tail)
            for item in shapes
        ]
        return pl.pallas_call(
            functools.partial(pack_windows_kernel, chips, planes, cols, kinds),
            grid=(comps,),
            in_specs=[
                pl.BlockSpec((snaps, 1, planes, width, depth), lambda comp: (0, comp, 0, 0, 0)),
            ],
            out_specs=specs,
            out_shape=[jax.ShapeDtypeStruct(item, kind) for item in shapes],
            scratch_shapes=[pltpu.VMEM((snaps * (width + 1), depth), jnp.float32)],
            compiler_params=params,
            name=name,
        )(here)

    away = range(1, chips)
    other = windows([(False, step) for step in away], own[0], "pack_other")
    mine = windows([(True, step) for step in away], other[0], "pack_mine")
    near = windows([(True, 0), (False, 0)], mine[0], "pack_near")
    return list(own), list(other), list(mine), list(near)


def coefficients(wide, metric, large, coef, first):
    comps, (_, planes, cols, depth) = 3, metric.shape
    width = large.shape[2]

    def rolled(comp, plane):
        values = large[comp, plane].astype(jnp.float32)
        return pltpu.roll(values, lax.rem(width + 1 - first, width), 0)

    def at(comp, plane):
        if 0 <= plane < planes:
            return rolled(comp, plane)[1 : cols + 1]
        side = 0 if plane < 0 else 1
        rows = [wide[side, comp, piece] for piece in range(wide.shape[2])]
        return jnp.concatenate(rows, axis=0).astype(jnp.float32)[:cols]

    for plane in range(planes):
        half_x, half_shear, half_y, half_z = [0.5 * metric[k, plane] for k in range(4)]
        step_y = [at(comp, plane + 1) - at(comp, plane - 1) for comp in range(comps)]
        step_z = [along_z(at(comp, plane)) for comp in range(2)]
        after = [rolled(comp, plane)[2 : cols + 2] for comp in (1, 2)]
        before = [rolled(comp, plane)[:cols] for comp in (1, 2)]
        rows = [
            half_x,
            half_shear,
            half_y,
            half_z,
            half_y * step_y[2] - half_z * step_z[1],
            half_z * step_z[0] - half_shear * step_y[2],
            half_shear * step_y[1] - half_y * step_y[0],
            half_x * after[0],
            half_x * before[0],
            half_x * after[1],
            half_x * before[1],
        ]
        for index, value in enumerate(rows):
            coef[plane, index] = value


def along_z(values):
    depth = values.shape[-1]
    return pltpu.roll(values, depth - 1, 1) - pltpu.roll(values, 1, 1)


def curl(get, row, mods, plane, col):
    def value(comp, plane_at, col_at):
        return get(comp, plane_at, col_at).astype(jnp.float32)

    gx, shear, gy, gz, ax, ay, az, v_after, v_before, w_after, w_before = row
    mod_before, mod_here, mod_after = mods
    dy_u, dy_v, dy_w = [value(k, plane + 1, col) - value(k, plane - 1, col) for k in range(3)]
    dz_u, dz_v = [along_z(value(k, plane, col)) for k in range(2)]
    dx_v, dx_w = [value(k, plane, col + 1) - value(k, plane, col - 1) for k in (1, 2)]
    around_x = gy * dy_w - gz * dz_v + mod_here * ax
    around_y = (
        gz * dz_u - gx * dx_w - shear * dy_w + mod_here * ay
        - (mod_after * w_after - mod_before * w_before)
    )
    around_z = (
        gx * dx_v + shear * dy_v - gy * dy_u + mod_here * az
        + (mod_after * v_after - mod_before * v_before)
    )
    return around_x, around_y, around_z


def split(value):
    top = value.astype(jnp.bfloat16)
    return top, (value - top.astype(jnp.float32)).astype(jnp.bfloat16)


def rows_of(chips, step, part, snaps):
    chip, core = whereabouts()
    owner = lax.rem(chip + chips - step, chips) * CORES + (1 - core if part else core)
    return pl.multiple_of(owner * snaps, snaps)


def curls(chips, field, steps, coef, amplitude, plane, cols, snaps, store):
    depth = amplitude.shape[2]
    for col in range(cols):
        row = [
            jnp.broadcast_to(coef[plane, index, pl.ds(col, 1), :], (snaps, depth))
            for index in range(11)
        ]
        for step in steps:
            for part in range(CORES):
                start = rows_of(chips, step, part, snaps)
                mods = [amplitude[col + k, pl.ds(start, snaps), :] for k in range(3)]
                get = functools.partial(field, step, part)
                for comp, value in enumerate(curl(get, row, mods, plane + 1, col + 1)):
                    store(comp, col, step, part, start, split(value))


def near_kernel(chips, planes, modulation, metric, large, *refs):
    own, (edge, other, pair, away, pair_other, away_other) = refs[:planes], refs[planes : planes + 6]
    early, coef, amplitude, mod, metric_mine, large_mine, wide, field, sem = refs[planes + 6 :]
    snaps, cols = early.shape[5], early.shape[2]
    extra = wide.shape[2]
    chip, core = whereabouts()
    first = pl.multiple_of((chip * CORES + core) * cols, 8)
    middle, left, right = pl.ds(1, cols), pl.ds(0, 1), pl.ds(cols + 1, 1)
    mine = pl.ds(core * cols, cols)
    moves = [
        (modulation, mod),
        (metric.at[:, :, pl.ds(first, cols)], metric_mine),
        (large, large_mine),
    ]
    for slot in range(planes):
        plane = plane_at(slot, planes) + 1
        moves += [
            (own[slot].at[:, mine], field.at[0, plane, :, middle]),
            (edge.at[:, pl.ds(2 * slot, 1)], field.at[0, plane, :, left]),
            (edge.at[:, pl.ds(2 * slot + 1, 1)], field.at[0, plane, :, right]),
            (other.at[:, slot], field.at[1, plane]),
        ]
    for slot, (close, far) in enumerate(((pair, pair_other), (away, away_other))):
        halo = halo_at(slot, planes)
        moves += [
            (close.at[:, mine], field.at[0, halo, :, middle]),
            (far, field.at[1, halo, :, middle]),
            (close.at[:, pl.ds(CORES * cols, extra)], wide.at[jnp.minimum(halo, 1)]),
        ]
    fetch_all(moves, sem.at[0])

    doubled = jnp.concatenate([mod[...], mod[...]], axis=1)
    doubled = pltpu.roll(doubled, lax.rem(doubled.shape[1] + 1 - first, doubled.shape[1]), 1)
    for col in range(cols + 2):
        amplitude[col] = jnp.broadcast_to(doubled[:, col : col + 1], amplitude.shape[1:])
    coefficients(wide, metric_mine, large_mine, coef, first)

    def tile(step, part, comp, plane, col):
        return field[part, plane, comp, col]

    for slot in range(planes):

        def store(comp, col, step, part, start, halves):
            for level in range(2):
                early[comp, slot, col, level, part] = halves[level]

        curls(chips, tile, [0], coef, amplitude, plane_at(slot, planes), cols, snaps, store)


def fetch_all(moves, sem):
    copies = [pltpu.make_async_copy(source, target, sem) for source, target in moves]
    for item in copies:
        item.start()
    for item in copies:
        item.wait()


def near_stage(modulation, metric, large, sources, chips, cols):
    everyone, _ = modulation.shape
    comps, planes, _, depth = large.shape
    snaps = everyone // (chips * CORES)
    extra = sources[0].shape[1] - CORES * cols
    whole = pl.BlockSpec(memory_space=pltpu.VMEM)
    return pl.pallas_call(
        functools.partial(near_kernel, chips, planes),
        in_specs=[pl.BlockSpec(memory_space=pl.ANY)] * (3 + len(sources)),
        out_specs=[whole] * 3,
        out_shape=[
            jax.ShapeDtypeStruct((comps, planes, cols, 2, CORES, snaps, depth), jnp.bfloat16),
            jax.ShapeDtypeStruct((planes, 11, cols, depth), jnp.float32),
            jax.ShapeDtypeStruct((cols + 2, everyone, depth), jnp.float32),
        ],
        scratch_shapes=[
            pltpu.VMEM(modulation.shape, modulation.dtype),
            pltpu.VMEM((4, planes, cols, depth), metric.dtype),
            pltpu.VMEM(large.shape, large.dtype),
            pltpu.VMEM((2, comps, extra, snaps, depth), large.dtype),
            pltpu.VMEM((CORES, planes + 2, comps, cols + 2, snaps, depth), large.dtype),
            pltpu.SemaphoreType.DMA((1,)),
        ],
        compiler_params=pltpu.CompilerParams(vmem_limit_bytes=VMEM_BYTES),
        cost_estimate=pl.CostEstimate(flops=0, bytes_accessed=8 << 20, transcendentals=0),
        name="near_stage",
    )(modulation, metric, large, *sources)


def far_kernel(chips, planes, slots, halo, coef, amplitude, early, before, *refs):
    sources, (parts, gram, field, total, sem) = list(refs[:-5]), refs[-5:]
    cols, snaps = early.shape[2], early.shape[5]
    everyone = amplitude.shape[1]
    middle, left, right = pl.ds(1, cols), pl.ds(0, 1), pl.ds(cols + 1, 1)
    moves = []
    for step in range(1, chips):
        own = [sources.pop(0) for _ in range(planes)]
        edge, beyond = sources.pop(0), sources.pop(0)
        for slot in range(planes):
            target = field.at[step - 1, plane_at(slot, planes) + 1]
            moves += [
                (own[slot], target.at[:, middle]),
                (edge.at[:, pl.ds(2 * slot, 1)], target.at[:, left]),
                (edge.at[:, pl.ds(2 * slot + 1, 1)], target.at[:, right]),
            ]
        moves.append((beyond, field.at[step - 1, halo_at(halo, planes), :, middle]))
    fetch_all(moves, sem.at[0])

    def tile(step, part, comp, plane, col):
        return field[step - 1, plane, comp, col, part * snaps : (part + 1) * snaps]

    total[...] = jnp.zeros_like(total)
    for index, slot in enumerate(slots):

        def store(comp, col, step, part, start, halves):
            for level in range(2):
                parts[comp, index, col, pl.ds(start + level * everyone, snaps), :] = halves[level]

        for part in range(CORES):
            start = rows_of(chips, 0, part, snaps)
            for comp in range(3):
                for col in range(cols):
                    halves = [early[comp, slot, col, level, part] for level in range(2)]
                    store(comp, col, 0, part, start, halves)
        steps = range(1, chips)
        plane = plane_at(slot, planes)
        curls(chips, tile, steps, coef, amplitude, plane, cols, snaps, store)
        for comp in range(3):
            for col in range(0, cols, 2):
                both = jnp.concatenate([parts[comp, index, col], parts[comp, index, col + 1]], 1)
                total[...] += lax.dot_general(
                    both, both, (((1,), (1,)), ((), ())), preferred_element_type=jnp.float32
                )
    gram[...] = before[...] + (
        total[:everyone, :everyone]
        + total[everyone:, everyone:]
        + (total[:everyone, everyone:] + total[everyone:, :everyone])
    )


def far_stage(coef, amplitude, early, before, sources, chips, slots, halo):
    comps, planes, cols, _, _, snaps, depth = early.shape
    everyone = snaps * chips * CORES
    whole = pl.BlockSpec(memory_space=pltpu.VMEM)
    return pl.pallas_call(
        functools.partial(far_kernel, chips, planes, slots, halo),
        in_specs=[whole] * 4 + [pl.BlockSpec(memory_space=pl.ANY)] * len(sources),
        out_specs=[whole, whole],
        out_shape=[
            jax.ShapeDtypeStruct((comps, len(slots), cols, 2 * everyone, depth), jnp.bfloat16),
            jax.ShapeDtypeStruct((everyone, everyone), jnp.float32),
        ],
        scratch_shapes=[
            pltpu.VMEM(
                (chips - 1, planes + 2, comps, cols + 2, CORES * snaps, depth), jnp.bfloat16
            ),
            pltpu.VMEM((2 * everyone, 2 * everyone), jnp.float32),
            pltpu.SemaphoreType.DMA((1,)),
        ],
        compiler_params=pltpu.CompilerParams(vmem_limit_bytes=VMEM_BYTES),
        cost_estimate=pl.CostEstimate(flops=0, bytes_accessed=8 << 20, transcendentals=0),
        name="far_stage",
    )(coef, amplitude, early, before, *sources)


def product(a, b):
    return jnp.dot(a, b, preferred_element_type=jnp.float32)


def whiten_kernel(count, gram, *refs):
    pieces, (out, slots, sems) = refs[:-3], refs[-3:]
    everyone = gram.shape[0]
    comps, cols, depth = pieces[0].shape[0], pieces[0].shape[2], pieces[0].shape[4]
    pitch = slots.shape[1] // everyone

    def dot(a, b):
        (a_top, a_rest), (b_top, b_rest) = split(a), split(b)
        cross = product(a_top, b_rest) + product(a_rest, b_top)
        return product(a_top, b_top) + cross

    correlation = gram[...] / count
    frob_scale = jnp.sqrt(jnp.sum(correlation * correlation, keepdims=True) + 1e-06)
    approx = correlation / frob_scale
    row = lax.broadcasted_iota(jnp.int32, (everyone, everyone), 0)
    col = lax.broadcasted_iota(jnp.int32, (everyone, everyone), 1)
    diagonal = jnp.where(row == col, 3.0, 0.0)
    factor = 0.5 * (diagonal - approx)
    inverse = factor
    for _ in range(1, NSITER):
        approx = dot(approx, factor)
        factor = 0.5 * (diagonal - dot(inverse, approx))
        inverse = dot(factor, inverse)
    top, rest = split(inverse / jnp.sqrt(frob_scale))
    left = jnp.concatenate([top, rest], axis=0)
    left = jnp.concatenate([left, left], axis=1)
    slot, copies = 0, []
    planes = sum(piece.shape[1] for piece in pieces)
    order = [1] + list(range(2, planes)) + [0]
    for piece in pieces:
        for index in range(piece.shape[1]):
            plane = plane_at(order.pop(0), planes)
            for comp in range(comps):
                for first in range(0, cols, 2):
                    both = [piece[comp, index, first], piece[comp, index, first + 1]]
                    both = jnp.concatenate(both, axis=1)
                    mixed = product(left, both)
                    mixed = mixed[:everyone] + mixed[everyone:]
                    for sub in range(2):
                        slots[slot, pl.ds(first + sub, everyone, stride=pitch), :] = mixed[
                            :, sub * depth : (sub + 1) * depth
                        ]
                source = slots.reshape(slots.shape[0], everyone, pitch, depth)
                copies.append(
                    pltpu.make_async_copy(
                        source.at[slot, :, pl.ds(0, cols)],
                        out.at[:, comp, plane],
                        sems.at[slot],
                    )
                )
                copies[-1].start()
                slot += 1
    for item in copies:
        item.wait()


def whiten(gram, pieces, count):
    everyone = gram.shape[0]
    comps, _, cols, _, depth = pieces[0].shape
    planes = sum(piece.shape[1] for piece in pieces)
    pitch = cols + 8 if (cols // 8) % 2 == 0 else cols
    whole = pl.BlockSpec(memory_space=pltpu.VMEM)
    return pl.pallas_call(
        functools.partial(whiten_kernel, count),
        in_specs=[whole] * (1 + len(pieces)),
        out_specs=pl.BlockSpec(memory_space=pl.ANY),
        out_shape=jax.ShapeDtypeStruct((everyone, comps, planes, cols, depth), jnp.float32),
        scratch_shapes=[
            pltpu.VMEM((comps * planes, everyone * pitch, depth), jnp.float32),
            pltpu.SemaphoreType.DMA((comps * planes,)),
        ],
        compiler_params=pltpu.CompilerParams(vmem_limit_bytes=VMEM_BYTES),
        name="whiten",
    )(gram, *pieces)


def to_chip(array, step):
    count = lax.axis_size("snap")
    pairs = [(i, (i + step * CORES) % count) for i in range(count)]
    return lax.ppermute(array, "snap", pairs)


def to_core(array):
    return lax.ppermute(array, "snap", [(i, i ^ 1) for i in range(lax.axis_size("snap"))])


def to_pair(array, first):
    count = lax.axis_size("slab")
    pairs = [(i, i + 1) for i in range(first, count - 1, 2)]
    return lax.ppermute(array, "slab", pairs + [(j, i) for i, j in pairs])


def all_sum(value):
    for axis in ("snap", "slab"):
        count = lax.axis_size(axis)
        if count & (count - 1):
            value = lax.psum(value, axis)
            continue
        stride = 1
        while stride < count:
            partners = [stride] if 2 * stride == count else [stride, 2 * stride, 3 * stride]
            received = [
                lax.ppermute(value, axis, [(i, i ^ k) for i in range(count)]) for k in partners
            ]
            value = sum(received, value)
            stride *= 1 + len(partners)
    return value


def per_device(flow, large_scale, modulation, metric):
    snap_count = lax.axis_size("snap")
    slab_count = lax.axis_size("slab")
    _, comps, planes, width, depth = flow.shape
    chips = snap_count // CORES
    cols = width // snap_count
    core = lax.rem(lax.axis_index("snap"), CORES)

    def half(array):
        return lax.dynamic_slice_in_dim(array, (1 - core) * cols, cols, 1)

    assert planes >= 2
    own, other, mine, near = pack(flow, large_scale, chips, cols)
    pair = to_pair(own[0], 0)
    outer, arrays = own[1], []
    for step in range(1, chips):
        both = jnp.concatenate([mine[step - 1], to_core(other[step - 1])], axis=3)
        outer, both = lax.optimization_barrier((outer, both))
        here = [to_chip(both[:, slot, 1:-1], step) for slot in range(planes)]
        edge = jnp.stack([both[:, :, 0], both[:, :, -1]], axis=2)
        edge = edge.reshape(comps, 2 * planes, *edge.shape[3:])
        edge, _ = lax.optimization_barrier((edge, here[0]))
        arrays.append((here + [to_chip(edge, step)], to_pair(here[0], 0), to_pair(here[1], 1)))
    away = to_pair(outer, 1)
    pair, away, _ = lax.optimization_barrier((pair, away, [here[:planes] for here, *_ in arrays]))
    sources = own + [near[0], to_core(near[1]), pair, away]
    sources += [to_core(half(pair)), to_core(half(away))]
    early, coef, amplitude = near_stage(modulation, metric, large_scale, sources, chips, cols)
    gram = jnp.zeros(modulation.shape[:1] * 2, jnp.float32)
    pieces = []
    for slots, halo in (((1,) + tuple(range(2, planes)), 1), ((0,), 0)):
        sources = []
        for here, *halos in arrays:
            sources += here + [halos[halo]]
        piece, gram = far_stage(coef, amplitude, early, gram, sources, chips, slots, halo)
        pieces.append(piece)
    return whiten(all_sum(gram), pieces, float(comps * planes * slab_count * width * depth))


def solution(mesh):
    return jax.shard_map(
        per_device,
        mesh=mesh,
        in_specs=(
            P("snap", None, "slab", None, None),
            P(None, "slab", None, None),
            P(),
            P(None, "slab", None, None),
        ),
        out_specs=P(None, None, "slab", "snap", None),
        check_vma=False,
    )
```

```python
import functools

import jax
import jax.numpy as jnp
from jax import lax
from jax.experimental import pallas as pl
from jax.experimental.pallas import tpu as pltpu
from jax.sharding import PartitionSpec as P

NSITER = 6
CORES = 2
VMEM_BYTES = 16 * 1024 * 1024


def whereabouts():
    place = lax.axis_index("snap")
    return lax.div(place, CORES), lax.rem(place, CORES)


def plane_at(slot, planes):
    upper = lax.rem(lax.axis_index("slab"), 2)
    if slot == 0:
        return (1 - upper) * (planes - 1)
    if slot == 1:
        return upper * (planes - 1)
    return slot - 1


def halo_at(slot, planes):
    upper = lax.rem(lax.axis_index("slab"), 2)
    return (1 - upper if slot == 0 else upper) * (planes + 1)


def spread(flat, pitch, snaps, values_of):
    for snap in range(snaps):
        values = values_of(snap)
        flat[pl.ds(snap * pitch, values.shape[0]), :] = values.astype(jnp.float32)

    def column(col):
        return flat[pl.ds(col, snaps, stride=pitch), :].astype(jnp.bfloat16)

    return column


def pack_own_kernel(planes, cols, flow, large, *refs):
    own, (near, flat, near_large, rows, sems) = refs[:-5], refs[-5:]
    snaps, comps, span = flow.shape[0], flow.shape[1], CORES * cols
    chip, core = whereabouts()
    first = pl.multiple_of(chip * span, span)
    copies = {}
    for slot in range(planes):
        for comp in range(comps):
            index = slot * comps + comp
            copies[index] = pltpu.make_async_copy(
                flow.at[:, comp, plane_at(slot, planes), pl.ds(first, span)],
                near.at[index],
                sems.at[index],
            )
            copies[index].start()
    fetch = pltpu.make_async_copy(large, near_large, sems.at[planes * comps])
    fetch.start()
    for slot in range(planes):
        for comp in range(comps):
            index = slot * comps + comp
            copies[index].wait()
            column = spread(flat, span + 1, snaps, lambda snap: near[index, snap])
            for col in range(span):
                own[slot][comp, col] = column(col)
    fetch.wait()
    rows[...] = near_large[...].astype(jnp.float32)
    start = pl.multiple_of(first + core * cols, 8)
    for slot in range(planes):
        for comp in range(comps):
            values = rows[comp, plane_at(slot, planes), pl.ds(start, cols), :]
            if cols % snaps:
                values = jnp.concatenate([values] * (snaps // cols), axis=0)
            for piece in range(values.shape[0] // snaps):
                tile = values[piece * snaps : (piece + 1) * snaps]
                own[slot][comp, span + piece] = tile.astype(jnp.bfloat16)


def pack_windows_kernel(chips, planes, cols, kinds, flow, *refs):
    outs, flat = refs[:-1], refs[-1]
    snaps, width = flow.shape[0], flow.shape[3]
    chip, core = whereabouts()
    for slot in range(planes):
        plane = plane_at(slot, planes)
        column = spread(flat, width + 1, snaps, lambda snap: flow[snap, 0, plane])
        for target, (mine, step) in zip(outs, kinds):
            part = core if mine else 1 - core
            start = lax.rem(chip + step, chips) * (CORES * cols) + part * cols
            left = column(lax.rem(start - 1 + width, width))
            right = column(lax.rem(start + cols, width))
            if mine and step == 0:
                target[0, 2 * slot] = left
                target[0, 2 * slot + 1] = right
                continue
            target[0, slot, 0] = left
            for col in range(cols):
                target[0, slot, col + 1] = column(start + col)
            target[0, slot, cols + 1] = right


def pack(flow, large, chips, cols):
    snaps, comps, planes, width, depth = flow.shape
    extra, span = -(-cols // snaps), CORES * cols
    kind = flow.dtype
    params = pltpu.CompilerParams(vmem_limit_bytes=VMEM_BYTES)
    def windows(kinds, after, name):
        here = flow if after is None else lax.optimization_barrier((flow, after))[0]

        def shape(mine, step):
            edge = mine and step == 0
            return (comps, 2 * planes) if edge else (comps, planes, cols + 2)

        shapes = [shape(*item) + (snaps, depth) for item in kinds]
        specs = [
            pl.BlockSpec((1,) + item[1:], lambda comp, tail=len(item) - 1: (comp,) + (0,) * tail)
            for item in shapes
        ]
        return pl.pallas_call(
            functools.partial(pack_windows_kernel, chips, planes, cols, kinds),
            grid=(comps,),
            in_specs=[
                pl.BlockSpec((snaps, 1, planes, width, depth), lambda comp: (0, comp, 0, 0, 0)),
            ],
            out_specs=specs,
            out_shape=[jax.ShapeDtypeStruct(item, kind) for item in shapes],
            scratch_shapes=[pltpu.VMEM((snaps * (width + 1), depth), jnp.float32)],
            compiler_params=params,
            name=name,
        )(here)

    away = range(1, chips)
    other = windows([(False, step) for step in away], None, "pack_other")
    lengths = [span + extra + 2] + [span + extra] * (planes - 1)
    own = pl.pallas_call(
        functools.partial(pack_own_kernel, planes, cols),
        in_specs=[pl.BlockSpec(memory_space=pltpu.HBM)] * 2,
        out_specs=[pl.BlockSpec(memory_space=pltpu.VMEM)] * planes,
        out_shape=[jax.ShapeDtypeStruct((comps, item, snaps, depth), kind) for item in lengths],
        scratch_shapes=[
            pltpu.VMEM((planes * comps, snaps, span, depth), kind),
            pltpu.VMEM((snaps * (span + 1), depth), jnp.float32),
            pltpu.VMEM(large.shape, kind),
            pltpu.VMEM(large.shape, jnp.float32),
            pltpu.SemaphoreType.DMA((planes * comps + 1,)),
        ],
        compiler_params=pltpu.CompilerParams(vmem_limit_bytes=VMEM_BYTES),
        name="pack_own",
    )(lax.optimization_barrier((flow, other[0]))[0], large)
    mine = windows([(True, step) for step in away], own[0], "pack_mine")
    near = windows([(True, 0), (False, 0)], mine[0], "pack_near")
    return list(own), list(other), list(mine), list(near)


def coefficients(wide, metric, large, coef, first):
    comps, (_, planes, cols, depth) = 3, metric.shape
    width = large.shape[2]

    def rolled(comp, plane):
        values = large[comp, plane].astype(jnp.float32)
        return pltpu.roll(values, lax.rem(width + 1 - first, width), 0)

    def at(comp, plane):
        if 0 <= plane < planes:
            return rolled(comp, plane)[1 : cols + 1]
        side = 0 if plane < 0 else 1
        rows = [wide[side, comp, piece] for piece in range(wide.shape[2])]
        return jnp.concatenate(rows, axis=0).astype(jnp.float32)[:cols]

    for plane in range(planes):
        half_x, half_shear, half_y, half_z = [0.5 * metric[k, plane] for k in range(4)]
        step_y = [at(comp, plane + 1) - at(comp, plane - 1) for comp in range(comps)]
        step_z = [along_z(at(comp, plane)) for comp in range(2)]
        after = [rolled(comp, plane)[2 : cols + 2] for comp in (1, 2)]
        before = [rolled(comp, plane)[:cols] for comp in (1, 2)]
        rows = [
            half_x,
            half_shear,
            half_y,
            half_z,
            half_y * step_y[2] - half_z * step_z[1],
            half_z * step_z[0] - half_shear * step_y[2],
            half_shear * step_y[1] - half_y * step_y[0],
            half_x * after[0],
            half_x * before[0],
            half_x * after[1],
            half_x * before[1],
        ]
        for index, value in enumerate(rows):
            coef[plane, index] = value


def along_z(values):
    depth = values.shape[-1]
    return pltpu.roll(values, depth - 1, 1) - pltpu.roll(values, 1, 1)


def curl(get, row, mods, plane, col):
    def value(comp, plane_at, col_at):
        return get(comp, plane_at, col_at).astype(jnp.float32)

    gx, shear, gy, gz, ax, ay, az, v_after, v_before, w_after, w_before = row
    mod_before, mod_here, mod_after = mods
    dy_u, dy_v, dy_w = [value(k, plane + 1, col) - value(k, plane - 1, col) for k in range(3)]
    dz_u, dz_v = [along_z(value(k, plane, col)) for k in range(2)]
    dx_v, dx_w = [value(k, plane, col + 1) - value(k, plane, col - 1) for k in (1, 2)]
    around_x = gy * dy_w - gz * dz_v + mod_here * ax
    around_y = (
        gz * dz_u - gx * dx_w - shear * dy_w + mod_here * ay
        - (mod_after * w_after - mod_before * w_before)
    )
    around_z = (
        gx * dx_v + shear * dy_v - gy * dy_u + mod_here * az
        + (mod_after * v_after - mod_before * v_before)
    )
    return around_x, around_y, around_z


def split(value):
    top = value.astype(jnp.bfloat16)
    return top, (value - top.astype(jnp.float32)).astype(jnp.bfloat16)


def rows_of(chips, step, part, snaps):
    chip, core = whereabouts()
    owner = lax.rem(chip + chips - step, chips) * CORES + (1 - core if part else core)
    return pl.multiple_of(owner * snaps, snaps)


def curls(chips, field, steps, coef, amplitude, plane, cols, snaps, store):
    depth = amplitude.shape[2]
    for col in range(cols):
        row = [
            jnp.broadcast_to(coef[plane, index, pl.ds(col, 1), :], (snaps, depth))
            for index in range(11)
        ]
        for step in steps:
            for part in range(CORES):
                start = rows_of(chips, step, part, snaps)
                mods = [amplitude[col + k, pl.ds(start, snaps), :] for k in range(3)]
                get = functools.partial(field, step, part)
                for comp, value in enumerate(curl(get, row, mods, plane + 1, col + 1)):
                    store(comp, col, step, part, start, split(value))


def near_kernel(chips, planes, modulation, metric, large, *refs):
    own, (edge, other, pair, away, pair_other, away_other) = refs[:planes], refs[planes : planes + 6]
    early, coef, amplitude, mod, metric_mine, large_mine, wide, field, sem = refs[planes + 6 :]
    snaps, cols = early.shape[5], early.shape[2]
    extra = wide.shape[2]
    chip, core = whereabouts()
    first = pl.multiple_of((chip * CORES + core) * cols, 8)
    middle, left, right = pl.ds(1, cols), pl.ds(0, 1), pl.ds(cols + 1, 1)
    mine = pl.ds(core * cols, cols)
    moves = [
        (modulation, mod),
        (metric.at[:, :, pl.ds(first, cols)], metric_mine),
        (large, large_mine),
    ]
    for slot in range(planes):
        plane = plane_at(slot, planes) + 1
        moves += [
            (own[slot].at[:, mine], field.at[0, plane, :, middle]),
            (edge.at[:, pl.ds(2 * slot, 1)], field.at[0, plane, :, left]),
            (edge.at[:, pl.ds(2 * slot + 1, 1)], field.at[0, plane, :, right]),
            (other.at[:, slot], field.at[1, plane]),
        ]
    for slot, (close, far) in enumerate(((pair, pair_other), (away, away_other))):
        halo = halo_at(slot, planes)
        moves += [
            (close.at[:, mine], field.at[0, halo, :, middle]),
            (far, field.at[1, halo, :, middle]),
            (close.at[:, pl.ds(CORES * cols, extra)], wide.at[jnp.minimum(halo, 1)]),
        ]
    fetch_all(moves, sem.at[0])

    doubled = jnp.concatenate([mod[...], mod[...]], axis=1)
    doubled = pltpu.roll(doubled, lax.rem(doubled.shape[1] + 1 - first, doubled.shape[1]), 1)
    for col in range(cols + 2):
        amplitude[col] = jnp.broadcast_to(doubled[:, col : col + 1], amplitude.shape[1:])
    coefficients(wide, metric_mine, large_mine, coef, first)

    def tile(step, part, comp, plane, col):
        return field[part, plane, comp, col]

    for slot in range(planes):

        def store(comp, col, step, part, start, halves):
            for level in range(2):
                early[comp, slot, col, level, part] = halves[level]

        curls(chips, tile, [0], coef, amplitude, plane_at(slot, planes), cols, snaps, store)


def fetch_all(moves, sem):
    copies = [pltpu.make_async_copy(source, target, sem) for source, target in moves]
    for item in copies:
        item.start()
    for item in copies:
        item.wait()


def near_stage(modulation, metric, large, sources, chips, cols):
    everyone, _ = modulation.shape
    comps, planes, _, depth = large.shape
    snaps = everyone // (chips * CORES)
    extra = sources[1].shape[1] - CORES * cols
    whole = pl.BlockSpec(memory_space=pltpu.VMEM)
    return pl.pallas_call(
        functools.partial(near_kernel, chips, planes),
        in_specs=[pl.BlockSpec(memory_space=pl.ANY)] * (3 + len(sources)),
        out_specs=[whole] * 3,
        out_shape=[
            jax.ShapeDtypeStruct((comps, planes, cols, 2, CORES, snaps, depth), jnp.bfloat16),
            jax.ShapeDtypeStruct((planes, 11, cols, depth), jnp.float32),
            jax.ShapeDtypeStruct((cols + 2, everyone, depth), jnp.float32),
        ],
        scratch_shapes=[
            pltpu.VMEM(modulation.shape, modulation.dtype),
            pltpu.VMEM((4, planes, cols, depth), metric.dtype),
            pltpu.VMEM(large.shape, large.dtype),
            pltpu.VMEM((2, comps, extra, snaps, depth), large.dtype),
            pltpu.VMEM((CORES, planes + 2, comps, cols + 2, snaps, depth), large.dtype),
            pltpu.SemaphoreType.DMA((1,)),
        ],
        compiler_params=pltpu.CompilerParams(vmem_limit_bytes=VMEM_BYTES),
        cost_estimate=pl.CostEstimate(flops=0, bytes_accessed=8 << 20, transcendentals=0),
        name="near_stage",
    )(modulation, metric, large, *sources)


def far_kernel(chips, planes, slots, halo, coef, amplitude, early, before, *refs):
    sources, (parts, gram, field, total, sem) = list(refs[:-5]), refs[-5:]
    cols, snaps = early.shape[2], early.shape[5]
    everyone = amplitude.shape[1]
    middle, left, right = pl.ds(1, cols), pl.ds(0, 1), pl.ds(cols + 1, 1)
    moves = []
    for step in range(1, chips):
        own = [sources.pop(0) for _ in range(planes)]
        edge, beyond = sources.pop(0), sources.pop(0)
        for slot in range(planes):
            target = field.at[step - 1, plane_at(slot, planes) + 1]
            moves += [
                (own[slot], target.at[:, middle]),
                (edge.at[:, pl.ds(2 * slot, 1)], target.at[:, left]),
                (edge.at[:, pl.ds(2 * slot + 1, 1)], target.at[:, right]),
            ]
        moves.append((beyond, field.at[step - 1, halo_at(halo, planes), :, middle]))
    fetch_all(moves, sem.at[0])

    def tile(step, part, comp, plane, col):
        return field[step - 1, plane, comp, col, part * snaps : (part + 1) * snaps]

    total[...] = jnp.zeros_like(total)
    for index, slot in enumerate(slots):

        def store(comp, col, step, part, start, halves):
            for level in range(2):
                parts[comp, index, col, pl.ds(start + level * everyone, snaps), :] = halves[level]

        for part in range(CORES):
            start = rows_of(chips, 0, part, snaps)
            for comp in range(3):
                for col in range(cols):
                    halves = [early[comp, slot, col, level, part] for level in range(2)]
                    store(comp, col, 0, part, start, halves)
        steps = range(1, chips)
        plane = plane_at(slot, planes)
        curls(chips, tile, steps, coef, amplitude, plane, cols, snaps, store)
        for comp in range(3):
            for col in range(0, cols, 2):
                both = jnp.concatenate([parts[comp, index, col], parts[comp, index, col + 1]], 1)
                total[...] += lax.dot_general(
                    both, both, (((1,), (1,)), ((), ())), preferred_element_type=jnp.float32
                )
    whole = (
        total[:everyone, :everyone]
        + total[everyone:, everyone:]
        + (total[:everyone, everyone:] + total[everyone:, :everyone])
    )
    gram[...] = before[...] + jnp.concatenate(
        [whole[: everyone // 2], whole[everyone // 2 :]], axis=1
    )


def far_stage(coef, amplitude, early, before, sources, chips, slots, halo):
    comps, planes, cols, _, _, snaps, depth = early.shape
    everyone = snaps * chips * CORES
    whole = pl.BlockSpec(memory_space=pltpu.VMEM)
    return pl.pallas_call(
        functools.partial(far_kernel, chips, planes, slots, halo),
        in_specs=[whole] * 4 + [pl.BlockSpec(memory_space=pl.ANY)] * len(sources),
        out_specs=[whole, whole],
        out_shape=[
            jax.ShapeDtypeStruct((comps, len(slots), cols, 2 * everyone, depth), jnp.bfloat16),
            jax.ShapeDtypeStruct((everyone // 2, 2 * everyone), jnp.float32),
        ],
        scratch_shapes=[
            pltpu.VMEM(
                (chips - 1, planes + 2, comps, cols + 2, CORES * snaps, depth), jnp.bfloat16
            ),
            pltpu.VMEM((2 * everyone, 2 * everyone), jnp.float32),
            pltpu.SemaphoreType.DMA((1,)),
        ],
        compiler_params=pltpu.CompilerParams(vmem_limit_bytes=VMEM_BYTES),
        cost_estimate=pl.CostEstimate(flops=0, bytes_accessed=8 << 20, transcendentals=0),
        name="far_stage",
    )(coef, amplitude, early, before, *sources)


def product(a, b):
    return jnp.dot(a, b, preferred_element_type=jnp.float32)


def whiten_kernel(count, gram, *refs):
    pieces, (out, slots, sems) = refs[:-3], refs[-3:]
    everyone = 2 * gram.shape[0]
    comps, cols, depth = pieces[0].shape[0], pieces[0].shape[2], pieces[0].shape[4]
    pitch = slots.shape[1] // everyone

    def dot(a, b):
        (a_top, a_rest), (b_top, b_rest) = split(a), split(b)
        cross = product(a_top, b_rest) + product(a_rest, b_top)
        return product(a_top, b_top) + cross

    correlation = jnp.concatenate([gram[:, :everyone], gram[:, everyone:]], axis=0) / count
    frob_scale = jnp.sqrt(jnp.sum(correlation * correlation, keepdims=True) + 1e-06)
    approx = correlation / frob_scale
    row = lax.broadcasted_iota(jnp.int32, (everyone, everyone), 0)
    col = lax.broadcasted_iota(jnp.int32, (everyone, everyone), 1)
    diagonal = jnp.where(row == col, 3.0, 0.0)
    factor = 0.5 * (diagonal - approx)
    inverse = factor
    for _ in range(1, NSITER):
        approx = dot(approx, factor)
        factor = 0.5 * (diagonal - dot(inverse, approx))
        inverse = dot(factor, inverse)
    top, rest = split(inverse / jnp.sqrt(frob_scale))
    left = jnp.concatenate([top, rest], axis=0)
    left = jnp.concatenate([left, left], axis=1)
    slot, copies = 0, []
    planes = sum(piece.shape[1] for piece in pieces)
    order = [1] + list(range(2, planes)) + [0]
    for piece in pieces:
        for index in range(piece.shape[1]):
            plane = plane_at(order.pop(0), planes)
            for comp in range(comps):
                for first in range(0, cols, 2):
                    both = [piece[comp, index, first], piece[comp, index, first + 1]]
                    both = jnp.concatenate(both, axis=1)
                    mixed = product(left, both)
                    mixed = mixed[:everyone] + mixed[everyone:]
                    for sub in range(2):
                        slots[slot, pl.ds(first + sub, everyone, stride=pitch), :] = mixed[
                            :, sub * depth : (sub + 1) * depth
                        ]
                source = slots.reshape(slots.shape[0], everyone, pitch, depth)
                copies.append(
                    pltpu.make_async_copy(
                        source.at[slot, :, pl.ds(0, cols)],
                        out.at[:, comp, plane],
                        sems.at[slot],
                    )
                )
                copies[-1].start()
                slot += 1
    for item in copies:
        item.wait()


def whiten(gram, pieces, count):
    everyone = 2 * gram.shape[0]
    comps, _, cols, _, depth = pieces[0].shape
    planes = sum(piece.shape[1] for piece in pieces)
    pitch = cols + 8 if (cols // 8) % 2 == 0 else cols
    whole = pl.BlockSpec(memory_space=pltpu.VMEM)
    return pl.pallas_call(
        functools.partial(whiten_kernel, count),
        in_specs=[whole] * (1 + len(pieces)),
        out_specs=pl.BlockSpec(memory_space=pl.ANY),
        out_shape=jax.ShapeDtypeStruct((everyone, comps, planes, cols, depth), jnp.float32),
        scratch_shapes=[
            pltpu.VMEM((comps * planes, everyone * pitch, depth), jnp.float32),
            pltpu.SemaphoreType.DMA((comps * planes,)),
        ],
        compiler_params=pltpu.CompilerParams(vmem_limit_bytes=VMEM_BYTES),
        name="whiten",
    )(gram, *pieces)


def to_chip(array, step):
    count = lax.axis_size("snap")
    pairs = [(i, (i + step * CORES) % count) for i in range(count)]
    return lax.ppermute(array, "snap", pairs)


def to_core(array):
    return lax.ppermute(array, "snap", [(i, i ^ 1) for i in range(lax.axis_size("snap"))])


def to_pair(array, first):
    count = lax.axis_size("slab")
    pairs = [(i, i + 1) for i in range(first, count - 1, 2)]
    return lax.ppermute(array, "slab", pairs + [(j, i) for i, j in pairs])


def all_sum(value):
    for axis in ("snap", "slab"):
        count = lax.axis_size(axis)
        if count & (count - 1):
            value = lax.psum(value, axis)
            continue
        stride = 1
        while stride < count:
            partners = [stride] if 2 * stride == count else [stride, 2 * stride, 3 * stride]
            received = [
                lax.ppermute(value, axis, [(i, i ^ k) for i in range(count)]) for k in partners
            ]
            value = sum(received, value)
            stride *= 1 + len(partners)
    return value


def per_device(flow, large_scale, modulation, metric):
    snap_count = lax.axis_size("snap")
    slab_count = lax.axis_size("slab")
    _, comps, planes, width, depth = flow.shape
    chips = snap_count // CORES
    cols = width // snap_count
    core = lax.rem(lax.axis_index("snap"), CORES)

    def half(array):
        return lax.dynamic_slice_in_dim(array, (1 - core) * cols, cols, 1)

    assert planes >= 2
    own, other, mine, near = pack(flow, large_scale, chips, cols)
    pair = to_pair(own[0], 0)
    outer, arrays = own[1], []
    for step in range(1, chips):
        both = jnp.concatenate([mine[step - 1], to_core(other[step - 1])], axis=3)
        outer, both = lax.optimization_barrier((outer, both))
        here = [to_chip(both[:, slot, 1:-1], step) for slot in range(planes)]
        edge = jnp.stack([both[:, :, 0], both[:, :, -1]], axis=2)
        edge = edge.reshape(comps, 2 * planes, *edge.shape[3:])
        edge, _ = lax.optimization_barrier((edge, here[0]))
        arrays.append((here + [to_chip(edge, step)], to_pair(here[0], 0), to_pair(here[1], 1)))
    away = to_pair(outer, 1)
    pair, away, _ = lax.optimization_barrier((pair, away, [here[:planes] for here, *_ in arrays]))
    sources = own + [near[0], to_core(near[1]), pair, away]
    sources += [to_core(half(pair)), to_core(half(away))]
    early, coef, amplitude = near_stage(modulation, metric, large_scale, sources, chips, cols)
    everyone = modulation.shape[0]
    gram = jnp.zeros((everyone // 2, 2 * everyone), jnp.float32)
    pieces = []
    for slots, halo in (((1,) + tuple(range(2, planes)), 1), ((0,), 0)):
        sources = []
        for here, *halos in arrays:
            sources += here + [halos[halo]]
        piece, gram = far_stage(coef, amplitude, early, gram, sources, chips, slots, halo)
        pieces.append(piece)
    return whiten(all_sum(gram), pieces, float(comps * planes * slab_count * width * depth))


def solution(mesh):
    return jax.shard_map(
        per_device,
        mesh=mesh,
        in_specs=(
            P("snap", None, "slab", None, None),
            P(None, "slab", None, None),
            P(),
            P(None, "slab", None, None),
        ),
        out_specs=P(None, None, "slab", "snap", None),
        check_vma=False,
    )
```

```python
import functools

import jax
import jax.numpy as jnp
from jax import lax
from jax.experimental import pallas as pl
from jax.experimental.pallas import tpu as pltpu
from jax.sharding import PartitionSpec as P

NSITER = 6
CORES = 2
VMEM_BYTES = 16 * 1024 * 1024


def whereabouts():
    place = lax.axis_index("snap")
    return lax.div(place, CORES), lax.rem(place, CORES)


def plane_at(slot, planes):
    upper = lax.rem(lax.axis_index("slab"), 2)
    if slot == 0:
        return (1 - upper) * (planes - 1)
    if slot == 1:
        return upper * (planes - 1)
    return slot - 1


def halo_at(slot, planes):
    upper = lax.rem(lax.axis_index("slab"), 2)
    return (1 - upper if slot == 0 else upper) * (planes + 1)


def spread(flat, pitch, snaps, values_of):
    for snap in range(snaps):
        values = values_of(snap)
        flat[pl.ds(snap * pitch, values.shape[0]), :] = values.astype(jnp.float32)

    def column(col):
        return flat[pl.ds(col, snaps, stride=pitch), :].astype(jnp.bfloat16)

    return column


def pack_own_kernel(planes, cols, flow, large, *refs):
    own, (near, flat, near_large, rows, sems) = refs[:-5], refs[-5:]
    snaps, comps, span = flow.shape[0], flow.shape[1], CORES * cols
    chip, core = whereabouts()
    first = pl.multiple_of(chip * span, span)
    copies = {}
    for slot in range(planes):
        for comp in range(comps):
            index = slot * comps + comp
            copies[index] = pltpu.make_async_copy(
                flow.at[:, comp, plane_at(slot, planes), pl.ds(first, span)],
                near.at[index],
                sems.at[index],
            )
            copies[index].start()
    fetch = pltpu.make_async_copy(large, near_large, sems.at[planes * comps])
    fetch.start()
    for slot in range(planes):
        for comp in range(comps):
            index = slot * comps + comp
            copies[index].wait()
            column = spread(flat, span + 1, snaps, lambda snap: near[index, snap])
            for col in range(span):
                own[slot][comp, col] = column(col)
    fetch.wait()
    rows[...] = near_large[...].astype(jnp.float32)
    start = pl.multiple_of(first + core * cols, 8)
    for slot in range(planes):
        for comp in range(comps):
            values = rows[comp, plane_at(slot, planes), pl.ds(start, cols), :]
            if cols % snaps:
                values = jnp.concatenate([values] * (snaps // cols), axis=0)
            for piece in range(values.shape[0] // snaps):
                tile = values[piece * snaps : (piece + 1) * snaps]
                own[slot][comp, span + piece] = tile.astype(jnp.bfloat16)


def pack_windows_kernel(chips, planes, cols, kinds, flow, *refs):
    outs, flat = refs[:-1], refs[-1]
    snaps, width = flow.shape[0], flow.shape[3]
    chip, core = whereabouts()
    for slot in range(planes):
        plane = plane_at(slot, planes)
        column = spread(flat, width + 1, snaps, lambda snap: flow[snap, 0, plane])
        for target, (mine, step) in zip(outs, kinds):
            part = core if mine else 1 - core
            start = lax.rem(chip + step, chips) * (CORES * cols) + part * cols
            left = column(lax.rem(start - 1 + width, width))
            right = column(lax.rem(start + cols, width))
            if mine and step == 0:
                target[0, 2 * slot] = left
                target[0, 2 * slot + 1] = right
                continue
            target[0, slot, 0] = left
            for col in range(cols):
                target[0, slot, col + 1] = column(start + col)
            target[0, slot, cols + 1] = right


def pack(flow, large, chips, cols):
    snaps, comps, planes, width, depth = flow.shape
    extra, span = -(-cols // snaps), CORES * cols
    kind = flow.dtype
    params = pltpu.CompilerParams(vmem_limit_bytes=VMEM_BYTES)
    def windows(kinds, after, name):
        here = flow if after is None else lax.optimization_barrier((flow, after))[0]

        def shape(mine, step):
            edge = mine and step == 0
            return (comps, 2 * planes) if edge else (comps, planes, cols + 2)

        shapes = [shape(*item) + (snaps, depth) for item in kinds]
        specs = [
            pl.BlockSpec((1,) + item[1:], lambda comp, tail=len(item) - 1: (comp,) + (0,) * tail)
            for item in shapes
        ]
        return pl.pallas_call(
            functools.partial(pack_windows_kernel, chips, planes, cols, kinds),
            grid=(comps,),
            in_specs=[
                pl.BlockSpec((snaps, 1, planes, width, depth), lambda comp: (0, comp, 0, 0, 0)),
            ],
            out_specs=specs,
            out_shape=[jax.ShapeDtypeStruct(item, kind) for item in shapes],
            scratch_shapes=[pltpu.VMEM((snaps * (width + 1), depth), jnp.float32)],
            compiler_params=params,
            name=name,
        )(here)

    away = range(1, chips)
    other = windows([(False, step) for step in away], None, "pack_other")
    lengths = [span + extra + 2] + [span + extra] * (planes - 1)
    own = pl.pallas_call(
        functools.partial(pack_own_kernel, planes, cols),
        in_specs=[pl.BlockSpec(memory_space=pltpu.HBM)] * 2,
        out_specs=[pl.BlockSpec(memory_space=pltpu.VMEM)] * planes,
        out_shape=[jax.ShapeDtypeStruct((comps, item, snaps, depth), kind) for item in lengths],
        scratch_shapes=[
            pltpu.VMEM((planes * comps, snaps, span, depth), kind),
            pltpu.VMEM((snaps * (span + 1), depth), jnp.float32),
            pltpu.VMEM(large.shape, kind),
            pltpu.VMEM(large.shape, jnp.float32),
            pltpu.SemaphoreType.DMA((planes * comps + 1,)),
        ],
        compiler_params=pltpu.CompilerParams(vmem_limit_bytes=VMEM_BYTES),
        name="pack_own",
    )(lax.optimization_barrier((flow, other[0]))[0], large)
    mine = windows([(True, step) for step in away], own[0], "pack_mine")
    near = windows([(True, 0), (False, 0)], mine[0], "pack_near")
    return list(own), list(other), list(mine), list(near)


def coefficients(wide, metric, large, coef, first):
    comps, (_, planes, cols, depth) = 3, metric.shape
    width = large.shape[2]

    def rolled(comp, plane):
        values = large[comp, plane].astype(jnp.float32)
        return pltpu.roll(values, lax.rem(width + 1 - first, width), 0)

    def at(comp, plane):
        if 0 <= plane < planes:
            return rolled(comp, plane)[1 : cols + 1]
        side = 0 if plane < 0 else 1
        rows = [wide[side, comp, piece] for piece in range(wide.shape[2])]
        return jnp.concatenate(rows, axis=0).astype(jnp.float32)[:cols]

    for plane in range(planes):
        half_x, half_shear, half_y, half_z = [0.5 * metric[k, plane] for k in range(4)]
        step_y = [at(comp, plane + 1) - at(comp, plane - 1) for comp in range(comps)]
        step_z = [along_z(at(comp, plane)) for comp in range(2)]
        after = [rolled(comp, plane)[2 : cols + 2] for comp in (1, 2)]
        before = [rolled(comp, plane)[:cols] for comp in (1, 2)]
        rows = [
            half_x,
            half_shear,
            half_y,
            half_z,
            half_y * step_y[2] - half_z * step_z[1],
            half_z * step_z[0] - half_shear * step_y[2],
            half_shear * step_y[1] - half_y * step_y[0],
            half_x * after[0],
            half_x * before[0],
            half_x * after[1],
            half_x * before[1],
        ]
        for index, value in enumerate(rows):
            coef[plane, index] = value


def along_z(values):
    depth = values.shape[-1]
    return pltpu.roll(values, depth - 1, 1) - pltpu.roll(values, 1, 1)


def curl(get, row, mods, plane, col, inner=None):
    def value(comp, plane_at, col_at):
        return get(comp, plane_at, col_at).astype(jnp.float32)

    gx, shear, gy, gz, ax, ay, az, v_after, v_before, w_after, w_before = row
    mod_before, mod_here, mod_after = mods
    if inner is None:
        steps = [value(k, plane + 1, col) - value(k, plane - 1, col) for k in range(3)]
    else:
        steps = [-value(k, inner, col) for k in range(3)]
    dy_u, dy_v, dy_w = steps
    dz_u, dz_v = [along_z(value(k, plane, col)) for k in range(2)]
    dx_v, dx_w = [value(k, plane, col + 1) - value(k, plane, col - 1) for k in (1, 2)]
    around_x = gy * dy_w - gz * dz_v + mod_here * ax
    around_y = (
        gz * dz_u - gx * dx_w - shear * dy_w + mod_here * ay
        - (mod_after * w_after - mod_before * w_before)
    )
    around_z = (
        gx * dx_v + shear * dy_v - gy * dy_u + mod_here * az
        + (mod_after * v_after - mod_before * v_before)
    )
    return around_x, around_y, around_z


def split(value):
    top = value.astype(jnp.bfloat16)
    return top, (value - top.astype(jnp.float32)).astype(jnp.bfloat16)


def rows_of(chips, step, part, snaps):
    chip, core = whereabouts()
    owner = lax.rem(chip + chips - step, chips) * CORES + (1 - core if part else core)
    return pl.multiple_of(owner * snaps, snaps)


def metric_rows(coef, plane, col, indices, snaps):
    depth = coef.shape[3]
    return [
        jnp.broadcast_to(coef[plane, index, pl.ds(col, 1), :], (snaps, depth)) for index in indices
    ]


def curls(chips, field, steps, coef, amplitude, plane, cols, snaps, store, upper=None):
    for col in range(cols):
        row = metric_rows(coef, plane, col, range(11), snaps)
        inner = None
        if upper is not None:
            sign = (1 - 2 * upper).astype(jnp.float32)
            row[1], row[2] = row[1] * sign, row[2] * sign
            inner = plane + 2 * upper
        for step in steps:
            for part in range(CORES):
                start = rows_of(chips, step, part, snaps)
                mods = [amplitude[col + k, pl.ds(start, snaps), :] for k in range(3)]
                get = functools.partial(field, step, part)
                values = curl(get, row, mods, plane + 1, col + 1, inner)
                for comp, value in enumerate(values):
                    store(comp, col, step, part, start, value)


def near_kernel(chips, planes, modulation, metric, large, *refs):
    own, (edge, other, pair, away, pair_other, away_other) = refs[:planes], refs[planes : planes + 6]
    early, coef, amplitude, mod, metric_mine, large_mine, wide, field, sem = refs[planes + 6 :]
    snaps, cols = early.shape[5], early.shape[2]
    extra = wide.shape[2]
    chip, core = whereabouts()
    first = pl.multiple_of((chip * CORES + core) * cols, 8)
    middle, left, right = pl.ds(1, cols), pl.ds(0, 1), pl.ds(cols + 1, 1)
    mine = pl.ds(core * cols, cols)
    moves = [
        (modulation, mod),
        (metric.at[:, :, pl.ds(first, cols)], metric_mine),
        (large, large_mine),
    ]
    for slot in range(planes):
        plane = plane_at(slot, planes) + 1
        moves += [
            (own[slot].at[:, mine], field.at[0, plane, :, middle]),
            (edge.at[:, pl.ds(2 * slot, 1)], field.at[0, plane, :, left]),
            (edge.at[:, pl.ds(2 * slot + 1, 1)], field.at[0, plane, :, right]),
            (other.at[:, slot], field.at[1, plane]),
        ]
    for slot, (close, far) in enumerate(((pair, pair_other), (away, away_other))):
        halo = halo_at(slot, planes)
        moves += [
            (close.at[:, mine], field.at[0, halo, :, middle]),
            (far, field.at[1, halo, :, middle]),
            (close.at[:, pl.ds(CORES * cols, extra)], wide.at[jnp.minimum(halo, 1)]),
        ]
    fetch_all(moves, sem.at[0])

    doubled = jnp.concatenate([mod[...], mod[...]], axis=1)
    doubled = pltpu.roll(doubled, lax.rem(doubled.shape[1] + 1 - first, doubled.shape[1]), 1)
    for col in range(cols + 2):
        amplitude[col] = jnp.broadcast_to(doubled[:, col : col + 1], amplitude.shape[1:])
    coefficients(wide, metric_mine, large_mine, coef, first)

    def tile(step, part, comp, plane, col):
        return field[part, plane, comp, col]

    for slot in range(planes):

        def store(comp, col, step, part, start, value):
            for level, half in enumerate(split(value)):
                early[comp, slot, col, level, part] = half

        curls(chips, tile, [0], coef, amplitude, plane_at(slot, planes), cols, snaps, store)


def fetch_all(moves, sem):
    copies = [pltpu.make_async_copy(source, target, sem) for source, target in moves]
    for item in copies:
        item.start()
    for item in copies:
        item.wait()


def near_stage(modulation, metric, large, sources, chips, cols):
    everyone, _ = modulation.shape
    comps, planes, _, depth = large.shape
    snaps = everyone // (chips * CORES)
    extra = sources[1].shape[1] - CORES * cols
    whole = pl.BlockSpec(memory_space=pltpu.VMEM)
    return pl.pallas_call(
        functools.partial(near_kernel, chips, planes),
        in_specs=[pl.BlockSpec(memory_space=pl.ANY)] * (3 + len(sources)),
        out_specs=[whole] * 3,
        out_shape=[
            jax.ShapeDtypeStruct((comps, planes, cols, 2, CORES, snaps, depth), jnp.bfloat16),
            jax.ShapeDtypeStruct((planes, 11, cols, depth), jnp.float32),
            jax.ShapeDtypeStruct((cols + 2, everyone, depth), jnp.float32),
        ],
        scratch_shapes=[
            pltpu.VMEM(modulation.shape, modulation.dtype),
            pltpu.VMEM((4, planes, cols, depth), metric.dtype),
            pltpu.VMEM(large.shape, large.dtype),
            pltpu.VMEM((2, comps, extra, snaps, depth), large.dtype),
            pltpu.VMEM((CORES, planes + 2, comps, cols + 2, snaps, depth), large.dtype),
            pltpu.SemaphoreType.DMA((1,)),
        ],
        compiler_params=pltpu.CompilerParams(vmem_limit_bytes=VMEM_BYTES),
        cost_estimate=pl.CostEstimate(flops=0, bytes_accessed=8 << 20, transcendentals=0),
        name="near_stage",
    )(modulation, metric, large, *sources)


def put(parts, index, comp, col, start, halves):
    everyone = parts.shape[3] // 2
    for level, half in enumerate(halves):
        rows = pl.ds(start + level * everyone, half.shape[0])
        parts[comp, index, col, rows, :] = half


def put_early(chips, early, slot, parts, index):
    cols, snaps = early.shape[2], early.shape[5]
    for part in range(CORES):
        start = rows_of(chips, 0, part, snaps)
        for comp in range(3):
            for col in range(cols):
                halves = [early[comp, slot, col, level, part] for level in range(2)]
                put(parts, index, comp, col, start, halves)


def add_products(parts, index, total):
    for comp in range(3):
        columns = [parts[comp, index, col] for col in range(parts.shape[2])]
        both = jnp.concatenate(columns, axis=1)
        total[...] += lax.dot_general(
            both,
            both[: total.shape[1]],
            (((1,), (1,)), ((), ())),
            preferred_element_type=jnp.float32,
        )


def folded(total):
    everyone = total.shape[1]
    cross = total[everyone:]
    whole = total[:everyone] + (cross + cross.T)
    return jnp.concatenate([whole[: everyone // 2], whole[everyone // 2 :]], axis=1)


def far_kernel(chips, planes, coef, amplitude, early, *refs):
    sources, (parts, gram, base, field, total, sem) = list(refs[:-6]), refs[-6:]
    cols, snaps = early.shape[2], early.shape[5]
    middle, left, right = pl.ds(1, cols), pl.ds(0, 1), pl.ds(cols + 1, 1)
    moves = []
    for step in range(1, chips):
        own = [sources.pop(0) for _ in range(planes)]
        edge, beyond = sources.pop(0), sources.pop(0)
        for slot in range(planes):
            target = field.at[step - 1, plane_at(slot, planes) + 1]
            moves += [
                (own[slot], target.at[:, middle]),
                (edge.at[:, pl.ds(2 * slot, 1)], target.at[:, left]),
                (edge.at[:, pl.ds(2 * slot + 1, 1)], target.at[:, right]),
            ]
        moves.append((beyond, field.at[step - 1, halo_at(1, planes), :, middle]))
    fetch_all(moves, sem.at[0])

    def tile(step, part, comp, plane, col):
        return field[step - 1, plane, comp, col, part * snaps : (part + 1) * snaps]

    total[...] = jnp.zeros_like(total)
    steps = range(1, chips)
    for index, slot in enumerate(range(1, planes)):

        def store(comp, col, step, part, start, value):
            put(parts, index, comp, col, start, split(value))

        put_early(chips, early, slot, parts, index)
        plane = plane_at(slot, planes)
        curls(chips, tile, steps, coef, amplitude, plane, cols, snaps, store)
        add_products(parts, index, total)
    gram[...] = folded(total)

    def store(comp, col, step, part, start, value):
        base[comp, step - 1, col, part * snaps : (part + 1) * snaps, :] = value

    upper = lax.rem(lax.axis_index("slab"), 2)
    plane = plane_at(0, planes)
    curls(chips, tile, steps, coef, amplitude, plane, cols, snaps, store, upper)


def last_kernel(chips, planes, coef, early, before, base, *refs):
    sources, (parts, gram, beyond, total, sem) = refs[:-5], refs[-5:]
    cols, snaps = early.shape[2], early.shape[5]
    fetch_all([(source, beyond.at[k]) for k, source in enumerate(sources)], sem.at[0])
    put_early(chips, early, 0, parts, 0)
    upper = lax.rem(lax.axis_index("slab"), 2)
    sign = (1 - 2 * upper).astype(jnp.float32)
    plane = plane_at(0, planes)
    for col in range(cols):
        shear, gy = [row * sign for row in metric_rows(coef, plane, col, (1, 2), snaps)]
        for step in range(1, chips):
            for part in range(CORES):
                rows = slice(part * snaps, (part + 1) * snaps)
                u, v, w = [beyond[step - 1, k, col, rows].astype(jnp.float32) for k in range(3)]
                added = (gy * w, -(shear * w), shear * v - gy * u)
                start = rows_of(chips, step, part, snaps)
                for comp in range(3):
                    value = base[comp, step - 1, col, rows, :] + added[comp]
                    put(parts, 0, comp, col, start, split(value))
    total[...] = jnp.zeros_like(total)
    add_products(parts, 0, total)
    gram[...] = before[...] + folded(total)


def stage(kernel, wholes, sources, outs, scratch, name):
    whole = pl.BlockSpec(memory_space=pltpu.VMEM)
    return pl.pallas_call(
        kernel,
        in_specs=[whole] * len(wholes) + [pl.BlockSpec(memory_space=pl.ANY)] * len(sources),
        out_specs=[whole] * len(outs),
        out_shape=[jax.ShapeDtypeStruct(*item) for item in outs],
        scratch_shapes=scratch + [pltpu.SemaphoreType.DMA((1,))],
        compiler_params=pltpu.CompilerParams(vmem_limit_bytes=VMEM_BYTES),
        cost_estimate=pl.CostEstimate(flops=0, bytes_accessed=8 << 20, transcendentals=0),
        name=name,
    )(*wholes, *sources)


def far_stage(coef, amplitude, early, sources, chips):
    comps, planes, cols, _, _, snaps, depth = early.shape
    group, everyone = CORES * snaps, snaps * chips * CORES
    kind = jnp.bfloat16
    return stage(
        functools.partial(far_kernel, chips, planes),
        [coef, amplitude, early],
        sources,
        [
            ((comps, planes - 1, cols, 2 * everyone, depth), kind),
            ((everyone // 2, 2 * everyone), jnp.float32),
            ((comps, chips - 1, cols, group, depth), jnp.float32),
        ],
        [
            pltpu.VMEM((chips - 1, planes + 2, comps, cols + 2, group, depth), kind),
            pltpu.VMEM((2 * everyone, everyone), jnp.float32),
        ],
        "far_stage",
    )


def last_stage(coef, early, gram, base, sources, chips):
    comps, planes, cols, _, _, snaps, depth = early.shape
    group, everyone = CORES * snaps, snaps * chips * CORES
    kind = jnp.bfloat16
    return stage(
        functools.partial(last_kernel, chips, planes),
        [coef, early, gram, base],
        sources,
        [((comps, 1, cols, 2 * everyone, depth), kind), (gram.shape, jnp.float32)],
        [
            pltpu.VMEM((chips - 1, comps, cols, group, depth), kind),
            pltpu.VMEM((2 * everyone, everyone), jnp.float32),
        ],
        "last_stage",
    )


def product(a, b):
    return jnp.dot(a, b, preferred_element_type=jnp.float32)


def whiten_kernel(count, gram, *refs):
    pieces, (out, slots, sems) = refs[:-3], refs[-3:]
    everyone = 2 * gram.shape[0]
    comps, cols, depth = pieces[0].shape[0], pieces[0].shape[2], pieces[0].shape[4]
    pitch = slots.shape[1] // everyone

    def dot(a, b):
        (a_top, a_rest), (b_top, b_rest) = split(a), split(b)
        cross = product(a_top, b_rest) + product(a_rest, b_top)
        return product(a_top, b_top) + cross

    correlation = jnp.concatenate([gram[:, :everyone], gram[:, everyone:]], axis=0) / count
    frob_scale = jnp.sqrt(jnp.sum(correlation * correlation, keepdims=True) + 1e-06)
    approx = correlation / frob_scale
    row = lax.broadcasted_iota(jnp.int32, (everyone, everyone), 0)
    col = lax.broadcasted_iota(jnp.int32, (everyone, everyone), 1)
    diagonal = jnp.where(row == col, 3.0, 0.0)
    factor = 0.5 * (diagonal - approx)
    inverse = factor
    for _ in range(1, NSITER):
        approx = dot(approx, factor)
        factor = 0.5 * (diagonal - dot(inverse, approx))
        inverse = dot(factor, inverse)
    top, rest = split(inverse / jnp.sqrt(frob_scale))
    left = jnp.concatenate([top, rest], axis=0)
    left = jnp.concatenate([left, left], axis=1)
    slot, copies = 0, []
    planes = sum(piece.shape[1] for piece in pieces)
    order = [1] + list(range(2, planes)) + [0]
    for piece in pieces:
        for index in range(piece.shape[1]):
            plane = plane_at(order.pop(0), planes)
            for comp in range(comps):
                for first in range(0, cols, 2):
                    both = [piece[comp, index, first], piece[comp, index, first + 1]]
                    both = jnp.concatenate(both, axis=1)
                    mixed = product(left, both)
                    mixed = mixed[:everyone] + mixed[everyone:]
                    for sub in range(2):
                        slots[slot, pl.ds(first + sub, everyone, stride=pitch), :] = mixed[
                            :, sub * depth : (sub + 1) * depth
                        ]
                source = slots.reshape(slots.shape[0], everyone, pitch, depth)
                copies.append(
                    pltpu.make_async_copy(
                        source.at[slot, :, pl.ds(0, cols)],
                        out.at[:, comp, plane],
                        sems.at[slot],
                    )
                )
                copies[-1].start()
                slot += 1
    for item in copies:
        item.wait()


def whiten(gram, pieces, count):
    everyone = 2 * gram.shape[0]
    comps, _, cols, _, depth = pieces[0].shape
    planes = sum(piece.shape[1] for piece in pieces)
    pitch = cols + 8 if (cols // 8) % 2 == 0 else cols
    whole = pl.BlockSpec(memory_space=pltpu.VMEM)
    return pl.pallas_call(
        functools.partial(whiten_kernel, count),
        in_specs=[whole] * (1 + len(pieces)),
        out_specs=pl.BlockSpec(memory_space=pl.ANY),
        out_shape=jax.ShapeDtypeStruct((everyone, comps, planes, cols, depth), jnp.float32),
        scratch_shapes=[
            pltpu.VMEM((comps * planes, everyone * pitch, depth), jnp.float32),
            pltpu.SemaphoreType.DMA((comps * planes,)),
        ],
        compiler_params=pltpu.CompilerParams(vmem_limit_bytes=VMEM_BYTES),
        name="whiten",
    )(gram, *pieces)


def to_chip(array, step):
    count = lax.axis_size("snap")
    pairs = [(i, (i + step * CORES) % count) for i in range(count)]
    return lax.ppermute(array, "snap", pairs)


def to_core(array):
    return lax.ppermute(array, "snap", [(i, i ^ 1) for i in range(lax.axis_size("snap"))])


def to_pair(array, first):
    count = lax.axis_size("slab")
    pairs = [(i, i + 1) for i in range(first, count - 1, 2)]
    return lax.ppermute(array, "slab", pairs + [(j, i) for i, j in pairs])


def all_sum(value):
    for axis in ("snap", "slab"):
        count = lax.axis_size(axis)
        if count & (count - 1):
            value = lax.psum(value, axis)
            continue
        stride = 1
        while stride < count:
            partners = [stride] if 2 * stride == count else [stride, 2 * stride, 3 * stride]
            received = [
                lax.ppermute(value, axis, [(i, i ^ k) for i in range(count)]) for k in partners
            ]
            value = sum(received, value)
            stride *= 1 + len(partners)
    return value


def per_device(flow, large_scale, modulation, metric):
    snap_count = lax.axis_size("snap")
    slab_count = lax.axis_size("slab")
    _, comps, planes, width, depth = flow.shape
    chips = snap_count // CORES
    cols = width // snap_count
    core = lax.rem(lax.axis_index("snap"), CORES)

    def half(array):
        return lax.dynamic_slice_in_dim(array, (1 - core) * cols, cols, 1)

    assert planes >= 2
    own, other, mine, near = pack(flow, large_scale, chips, cols)
    pair = to_pair(own[0], 0)
    outer, arrays = own[1], []
    for step in range(1, chips):
        both = jnp.concatenate([mine[step - 1], to_core(other[step - 1])], axis=3)
        outer, both = lax.optimization_barrier((outer, both))
        here = [to_chip(both[:, slot, 1:-1], step) for slot in range(planes)]
        edge = jnp.stack([both[:, :, 0], both[:, :, -1]], axis=2)
        edge = edge.reshape(comps, 2 * planes, *edge.shape[3:])
        edge, _ = lax.optimization_barrier((edge, here[0]))
        arrays.append((here + [to_chip(edge, step)], to_pair(here[0], 0), to_pair(here[1], 1)))
    away = to_pair(outer, 1)
    pair, away, _ = lax.optimization_barrier((pair, away, [here[:planes] for here, *_ in arrays]))
    sources = own + [near[0], to_core(near[1]), pair, away]
    sources += [to_core(half(pair)), to_core(half(away))]
    early, coef, amplitude = near_stage(modulation, metric, large_scale, sources, chips, cols)
    sources = []
    for here, _, outer_halo in arrays:
        sources += here + [outer_halo]
    far, gram, base = far_stage(coef, amplitude, early, sources, chips)
    sources = [inner_halo for _, inner_halo, _ in arrays]
    last, gram = last_stage(coef, early, gram, base, sources, chips)
    pieces = [far, last]
    return whiten(all_sum(gram), pieces, float(comps * planes * slab_count * width * depth))


def solution(mesh):
    return jax.shard_map(
        per_device,
        mesh=mesh,
        in_specs=(
            P("snap", None, "slab", None, None),
            P(None, "slab", None, None),
            P(),
            P(None, "slab", None, None),
        ),
        out_specs=P(None, None, "slab", "snap", None),
        check_vma=False,
    )
```

```python
import functools

import jax
import jax.numpy as jnp
from jax import lax
from jax.experimental import pallas as pl
from jax.experimental.pallas import tpu as pltpu
from jax.sharding import PartitionSpec as P

NSITER = 6
CORES = 2
VMEM_BYTES = 16 * 1024 * 1024


def whereabouts():
    place = lax.axis_index("snap")
    return lax.div(place, CORES), lax.rem(place, CORES)


def plane_at(slot, planes):
    upper = lax.rem(lax.axis_index("slab"), 2)
    if slot == 0:
        return (1 - upper) * (planes - 1)
    if slot == 1:
        return upper * (planes - 1)
    return slot - 1


def halo_at(slot, planes):
    upper = lax.rem(lax.axis_index("slab"), 2)
    return (1 - upper if slot == 0 else upper) * (planes + 1)


def spread(flat, pitch, snaps, values_of):
    for snap in range(snaps):
        values = values_of(snap)
        flat[pl.ds(snap * pitch, values.shape[0]), :] = values.astype(jnp.float32)

    def column(col):
        return flat[pl.ds(col, snaps, stride=pitch), :].astype(jnp.bfloat16)

    return column


def pack_own_kernel(planes, cols, flow, large, *refs):
    own, (near, flat, near_large, rows, sems) = refs[:-5], refs[-5:]
    snaps, comps, span = flow.shape[0], flow.shape[1], CORES * cols
    chip, core = whereabouts()
    first = pl.multiple_of(chip * span, span)
    copies = {}
    for slot in range(planes):
        for comp in range(comps):
            index = slot * comps + comp
            copies[index] = pltpu.make_async_copy(
                flow.at[:, comp, plane_at(slot, planes), pl.ds(first, span)],
                near.at[index],
                sems.at[index],
            )
            copies[index].start()
    fetch = pltpu.make_async_copy(large, near_large, sems.at[planes * comps])
    fetch.start()
    for slot in range(planes):
        for comp in range(comps):
            index = slot * comps + comp
            copies[index].wait()
            column = spread(flat, span + 1, snaps, lambda snap: near[index, snap])
            for col in range(span):
                own[slot][comp, col] = column(col)
    fetch.wait()
    rows[...] = near_large[...].astype(jnp.float32)
    start = pl.multiple_of(first + core * cols, 8)
    for slot in range(planes):
        for comp in range(comps):
            values = rows[comp, plane_at(slot, planes), pl.ds(start, cols), :]
            if cols % snaps:
                values = jnp.concatenate([values] * (snaps // cols), axis=0)
            for piece in range(values.shape[0] // snaps):
                tile = values[piece * snaps : (piece + 1) * snaps]
                own[slot][comp, span + piece] = tile.astype(jnp.bfloat16)


def pack_windows_kernel(chips, planes, cols, kinds, flow, *refs):
    outs, flat = refs[:-1], refs[-1]
    snaps, width = flow.shape[0], flow.shape[3]
    chip, core = whereabouts()
    for slot in range(planes):
        plane = plane_at(slot, planes)
        column = spread(flat, width + 1, snaps, lambda snap: flow[snap, 0, plane])
        for target, (mine, step) in zip(outs, kinds):
            part = core if mine else 1 - core
            start = lax.rem(chip + step, chips) * (CORES * cols) + part * cols
            left = column(lax.rem(start - 1 + width, width))
            right = column(lax.rem(start + cols, width))
            if mine and step == 0:
                target[0, 2 * slot] = left
                target[0, 2 * slot + 1] = right
                continue
            target[0, slot, 0] = left
            for col in range(cols):
                target[0, slot, col + 1] = column(start + col)
            target[0, slot, cols + 1] = right


def pack(flow, large, chips, cols):
    snaps, comps, planes, width, depth = flow.shape
    extra, span = -(-cols // snaps), CORES * cols
    kind = flow.dtype
    params = pltpu.CompilerParams(vmem_limit_bytes=VMEM_BYTES)
    def windows(kinds, after, name):
        here = flow if after is None else lax.optimization_barrier((flow, after))[0]

        def shape(mine, step):
            edge = mine and step == 0
            return (comps, 2 * planes) if edge else (comps, planes, cols + 2)

        shapes = [shape(*item) + (snaps, depth) for item in kinds]
        specs = [
            pl.BlockSpec((1,) + item[1:], lambda comp, tail=len(item) - 1: (comp,) + (0,) * tail)
            for item in shapes
        ]
        return pl.pallas_call(
            functools.partial(pack_windows_kernel, chips, planes, cols, kinds),
            grid=(comps,),
            in_specs=[
                pl.BlockSpec((snaps, 1, planes, width, depth), lambda comp: (0, comp, 0, 0, 0)),
            ],
            out_specs=specs,
            out_shape=[jax.ShapeDtypeStruct(item, kind) for item in shapes],
            scratch_shapes=[pltpu.VMEM((snaps * (width + 1), depth), jnp.float32)],
            compiler_params=params,
            name=name,
        )(here)

    away = range(1, chips)
    other = windows([(False, step) for step in away], None, "pack_other")
    lengths = [span + extra] + [span + extra] * (planes - 1)
    own = pl.pallas_call(
        functools.partial(pack_own_kernel, planes, cols),
        in_specs=[pl.BlockSpec(memory_space=pltpu.HBM)] * 2,
        out_specs=[pl.BlockSpec(memory_space=pltpu.VMEM)] * planes,
        out_shape=[jax.ShapeDtypeStruct((comps, item, snaps, depth), kind) for item in lengths],
        scratch_shapes=[
            pltpu.VMEM((planes * comps, snaps, span, depth), kind),
            pltpu.VMEM((snaps * (span + 1), depth), jnp.float32),
            pltpu.VMEM(large.shape, kind),
            pltpu.VMEM(large.shape, jnp.float32),
            pltpu.SemaphoreType.DMA((planes * comps + 1,)),
        ],
        compiler_params=pltpu.CompilerParams(vmem_limit_bytes=VMEM_BYTES),
        name="pack_own",
    )(lax.optimization_barrier((flow, other[0]))[0], large)
    mine = windows([(True, step) for step in away], own[0], "pack_mine")
    near = windows([(True, 0), (False, 0)], mine[0], "pack_near")
    return list(own), list(other), list(mine), list(near)


def coefficients(wide, metric, large, coef, first):
    comps, (_, planes, cols, depth) = 3, metric.shape
    width = large.shape[2]

    def rolled(comp, plane):
        values = large[comp, plane].astype(jnp.float32)
        return pltpu.roll(values, lax.rem(width + 1 - first, width), 0)

    def at(comp, plane):
        if 0 <= plane < planes:
            return rolled(comp, plane)[1 : cols + 1]
        side = 0 if plane < 0 else 1
        rows = [wide[side, comp, piece] for piece in range(wide.shape[2])]
        return jnp.concatenate(rows, axis=0).astype(jnp.float32)[:cols]

    for plane in range(planes):
        half_x, half_shear, half_y, half_z = [0.5 * metric[k, plane] for k in range(4)]
        step_y = [at(comp, plane + 1) - at(comp, plane - 1) for comp in range(comps)]
        step_z = [along_z(at(comp, plane)) for comp in range(2)]
        after = [rolled(comp, plane)[2 : cols + 2] for comp in (1, 2)]
        before = [rolled(comp, plane)[:cols] for comp in (1, 2)]
        rows = [
            half_x,
            half_shear,
            half_y,
            half_z,
            half_y * step_y[2] - half_z * step_z[1],
            half_z * step_z[0] - half_shear * step_y[2],
            half_shear * step_y[1] - half_y * step_y[0],
            half_x * after[0],
            half_x * before[0],
            half_x * after[1],
            half_x * before[1],
        ]
        for index, value in enumerate(rows):
            coef[plane, index] = value


def along_z(values):
    depth = values.shape[-1]
    return pltpu.roll(values, depth - 1, 1) - pltpu.roll(values, 1, 1)


def curl(get, row, mods, plane, col, inner=None):
    def value(comp, plane_at, col_at):
        return get(comp, plane_at, col_at).astype(jnp.float32)

    gx, shear, gy, gz, ax, ay, az, v_after, v_before, w_after, w_before = row
    mod_before, mod_here, mod_after = mods
    if inner is None:
        steps = [value(k, plane + 1, col) - value(k, plane - 1, col) for k in range(3)]
    else:
        steps = [-value(k, inner, col) for k in range(3)]
    dy_u, dy_v, dy_w = steps
    dz_u, dz_v = [along_z(value(k, plane, col)) for k in range(2)]
    dx_v, dx_w = [value(k, plane, col + 1) - value(k, plane, col - 1) for k in (1, 2)]
    around_x = gy * dy_w - gz * dz_v + mod_here * ax
    around_y = (
        gz * dz_u - gx * dx_w - shear * dy_w + mod_here * ay
        - (mod_after * w_after - mod_before * w_before)
    )
    around_z = (
        gx * dx_v + shear * dy_v - gy * dy_u + mod_here * az
        + (mod_after * v_after - mod_before * v_before)
    )
    return around_x, around_y, around_z


def split(value):
    top = value.astype(jnp.bfloat16)
    return top, (value - top.astype(jnp.float32)).astype(jnp.bfloat16)


def rows_of(chips, step, part, snaps):
    chip, core = whereabouts()
    owner = lax.rem(chip + chips - step, chips) * CORES + (1 - core if part else core)
    return pl.multiple_of(owner * snaps, snaps)


def metric_rows(coef, plane, col, indices, snaps):
    depth = coef.shape[3]
    return [
        jnp.broadcast_to(coef[plane, index, pl.ds(col, 1), :], (snaps, depth)) for index in indices
    ]


def curls(chips, field, steps, coef, amplitude, plane, cols, snaps, store, upper=None):
    for col in range(cols):
        row = metric_rows(coef, plane, col, range(11), snaps)
        inner = None
        if upper is not None:
            sign = (1 - 2 * upper).astype(jnp.float32)
            row[1], row[2] = row[1] * sign, row[2] * sign
            inner = plane + 2 * upper
        for step in steps:
            for part in range(CORES):
                start = rows_of(chips, step, part, snaps)
                mods = [amplitude[col + k, pl.ds(start, snaps), :] for k in range(3)]
                get = functools.partial(field, step, part)
                values = curl(get, row, mods, plane + 1, col + 1, inner)
                for comp, value in enumerate(values):
                    store(comp, col, step, part, start, value)


def near_kernel(chips, planes, modulation, metric, large, *refs):
    own, (edge, other, pair, away, pair_other, away_other) = refs[:planes], refs[planes : planes + 6]
    early, coef, amplitude, mod, metric_mine, large_mine, wide, field, sem = refs[planes + 6 :]
    snaps, cols = early.shape[5], early.shape[2]
    extra = wide.shape[2]
    chip, core = whereabouts()
    first = pl.multiple_of((chip * CORES + core) * cols, 8)
    middle, left, right = pl.ds(1, cols), pl.ds(0, 1), pl.ds(cols + 1, 1)
    mine = pl.ds(core * cols, cols)
    moves = [
        (modulation, mod),
        (metric.at[:, :, pl.ds(first, cols)], metric_mine),
        (large, large_mine),
    ]
    for slot in range(planes):
        plane = plane_at(slot, planes) + 1
        moves += [
            (own[slot].at[:, mine], field.at[0, plane, :, middle]),
            (edge.at[:, pl.ds(2 * slot, 1)], field.at[0, plane, :, left]),
            (edge.at[:, pl.ds(2 * slot + 1, 1)], field.at[0, plane, :, right]),
            (other.at[:, slot], field.at[1, plane]),
        ]
    for slot, (close, far) in enumerate(((pair, pair_other), (away, away_other))):
        halo = halo_at(slot, planes)
        moves += [
            (close.at[:, mine], field.at[0, halo, :, middle]),
            (far, field.at[1, halo, :, middle]),
            (close.at[:, pl.ds(CORES * cols, extra)], wide.at[jnp.minimum(halo, 1)]),
        ]
    fetch_all(moves, sem.at[0])

    doubled = jnp.concatenate([mod[...], mod[...]], axis=1)
    doubled = pltpu.roll(doubled, lax.rem(doubled.shape[1] + 1 - first, doubled.shape[1]), 1)
    for col in range(cols + 2):
        amplitude[col] = jnp.broadcast_to(doubled[:, col : col + 1], amplitude.shape[1:])
    coefficients(wide, metric_mine, large_mine, coef, first)

    def tile(step, part, comp, plane, col):
        return field[part, plane, comp, col]

    for slot in range(planes):

        def store(comp, col, step, part, start, value):
            for level, half in enumerate(split(value)):
                early[comp, slot, col, level, part] = half

        curls(chips, tile, [0], coef, amplitude, plane_at(slot, planes), cols, snaps, store)


def fetch_all(moves, sem):
    copies = [pltpu.make_async_copy(source, target, sem) for source, target in moves]
    for item in copies:
        item.start()
    for item in copies:
        item.wait()


def near_stage(modulation, metric, large, sources, chips, cols):
    everyone, _ = modulation.shape
    comps, planes, _, depth = large.shape
    snaps = everyone // (chips * CORES)
    extra = sources[1].shape[1] - CORES * cols
    whole = pl.BlockSpec(memory_space=pltpu.VMEM)
    return pl.pallas_call(
        functools.partial(near_kernel, chips, planes),
        in_specs=[pl.BlockSpec(memory_space=pl.ANY)] * (3 + len(sources)),
        out_specs=[whole] * 3,
        out_shape=[
            jax.ShapeDtypeStruct((comps, planes, cols, 2, CORES, snaps, depth), jnp.bfloat16),
            jax.ShapeDtypeStruct((planes, 11, cols, depth), jnp.float32),
            jax.ShapeDtypeStruct((cols + 2, everyone, depth), jnp.float32),
        ],
        scratch_shapes=[
            pltpu.VMEM(modulation.shape, modulation.dtype),
            pltpu.VMEM((4, planes, cols, depth), metric.dtype),
            pltpu.VMEM(large.shape, large.dtype),
            pltpu.VMEM((2, comps, extra, snaps, depth), large.dtype),
            pltpu.VMEM((CORES, planes + 2, comps, cols + 2, snaps, depth), large.dtype),
            pltpu.SemaphoreType.DMA((1,)),
        ],
        compiler_params=pltpu.CompilerParams(vmem_limit_bytes=VMEM_BYTES),
        cost_estimate=pl.CostEstimate(flops=0, bytes_accessed=8 << 20, transcendentals=0),
        name="near_stage",
    )(modulation, metric, large, *sources)


def put(parts, index, comp, col, start, halves):
    everyone = parts.shape[3] // 2
    for level, half in enumerate(halves):
        rows = pl.ds(start + level * everyone, half.shape[0])
        parts[comp, index, col, rows, :] = half


def put_early(chips, early, slot, parts, index):
    cols, snaps = early.shape[2], early.shape[5]
    for part in range(CORES):
        start = rows_of(chips, 0, part, snaps)
        for comp in range(3):
            for col in range(cols):
                halves = [early[comp, slot, col, level, part] for level in range(2)]
                put(parts, index, comp, col, start, halves)


def add_products(parts, index, total):
    for comp in range(3):
        columns = [parts[comp, index, col] for col in range(parts.shape[2])]
        both = jnp.concatenate(columns, axis=1)
        total[...] += lax.dot_general(
            both,
            both[: total.shape[1]],
            (((1,), (1,)), ((), ())),
            preferred_element_type=jnp.float32,
        )


def folded(total):
    everyone = total.shape[1]
    cross = total[everyone:]
    whole = total[:everyone] + (cross + cross.T)
    return jnp.concatenate([whole[: everyone // 2], whole[everyone // 2 :]], axis=1)


def far_kernel(chips, planes, coef, amplitude, early, *refs):
    sources, (parts, gram, base, field, total, sem) = list(refs[:-6]), refs[-6:]
    cols, snaps = early.shape[2], early.shape[5]
    middle, left, right = pl.ds(1, cols), pl.ds(0, 1), pl.ds(cols + 1, 1)
    moves = []
    for step in range(1, chips):
        own = [sources.pop(0) for _ in range(planes)]
        edge, beyond = sources.pop(0), sources.pop(0)
        for slot in range(planes):
            target = field.at[step - 1, plane_at(slot, planes) + 1]
            moves += [
                (own[slot], target.at[:, middle]),
                (edge.at[:, pl.ds(2 * slot, 1)], target.at[:, left]),
                (edge.at[:, pl.ds(2 * slot + 1, 1)], target.at[:, right]),
            ]
        moves.append((beyond, field.at[step - 1, halo_at(1, planes), :, middle]))
    fetch_all(moves, sem.at[0])

    def tile(step, part, comp, plane, col):
        return field[step - 1, plane, comp, col, part * snaps : (part + 1) * snaps]

    total[...] = jnp.zeros_like(total)
    steps = range(1, chips)
    for index, slot in enumerate(range(1, planes)):

        def store(comp, col, step, part, start, value):
            put(parts, index, comp, col, start, split(value))

        put_early(chips, early, slot, parts, index)
        plane = plane_at(slot, planes)
        curls(chips, tile, steps, coef, amplitude, plane, cols, snaps, store)
        add_products(parts, index, total)
    gram[...] = folded(total)

    def store(comp, col, step, part, start, value):
        base[comp, step - 1, col, part * snaps : (part + 1) * snaps, :] = value

    upper = lax.rem(lax.axis_index("slab"), 2)
    plane = plane_at(0, planes)
    curls(chips, tile, steps, coef, amplitude, plane, cols, snaps, store, upper)


def last_kernel(chips, planes, coef, early, before, base, *refs):
    sources, (parts, gram, beyond, total, sem) = refs[:-5], refs[-5:]
    cols, snaps = early.shape[2], early.shape[5]
    fetch_all([(source, beyond.at[k]) for k, source in enumerate(sources)], sem.at[0])
    put_early(chips, early, 0, parts, 0)
    upper = lax.rem(lax.axis_index("slab"), 2)
    sign = (1 - 2 * upper).astype(jnp.float32)
    plane = plane_at(0, planes)
    for col in range(cols):
        shear, gy = [row * sign for row in metric_rows(coef, plane, col, (1, 2), snaps)]
        for step in range(1, chips):
            for part in range(CORES):
                rows = slice(part * snaps, (part + 1) * snaps)
                u, v, w = [beyond[step - 1, k, col, rows].astype(jnp.float32) for k in range(3)]
                added = (gy * w, -(shear * w), shear * v - gy * u)
                start = rows_of(chips, step, part, snaps)
                for comp in range(3):
                    value = base[comp, step - 1, col, rows, :] + added[comp]
                    put(parts, 0, comp, col, start, split(value))
    total[...] = jnp.zeros_like(total)
    add_products(parts, 0, total)
    gram[...] = before[...] + folded(total)


def stage(kernel, wholes, sources, outs, scratch, name):
    whole = pl.BlockSpec(memory_space=pltpu.VMEM)
    return pl.pallas_call(
        kernel,
        in_specs=[whole] * len(wholes) + [pl.BlockSpec(memory_space=pl.ANY)] * len(sources),
        out_specs=[whole] * len(outs),
        out_shape=[jax.ShapeDtypeStruct(*item) for item in outs],
        scratch_shapes=scratch + [pltpu.SemaphoreType.DMA((1,))],
        compiler_params=pltpu.CompilerParams(vmem_limit_bytes=VMEM_BYTES),
        cost_estimate=pl.CostEstimate(flops=0, bytes_accessed=8 << 20, transcendentals=0),
        name=name,
    )(*wholes, *sources)


def far_stage(coef, amplitude, early, sources, chips):
    comps, planes, cols, _, _, snaps, depth = early.shape
    group, everyone = CORES * snaps, snaps * chips * CORES
    kind = jnp.bfloat16
    return stage(
        functools.partial(far_kernel, chips, planes),
        [coef, amplitude, early],
        sources,
        [
            ((comps, planes - 1, cols, 2 * everyone, depth), kind),
            ((everyone // 2, 2 * everyone), jnp.float32),
            ((comps, chips - 1, cols, group, depth), jnp.float32),
        ],
        [
            pltpu.VMEM((chips - 1, planes + 2, comps, cols + 2, group, depth), kind),
            pltpu.VMEM((2 * everyone, everyone), jnp.float32),
        ],
        "far_stage",
    )


def last_stage(coef, early, gram, base, sources, chips):
    comps, planes, cols, _, _, snaps, depth = early.shape
    group, everyone = CORES * snaps, snaps * chips * CORES
    kind = jnp.bfloat16
    return stage(
        functools.partial(last_kernel, chips, planes),
        [coef, early, gram, base],
        sources,
        [((comps, 1, cols, 2 * everyone, depth), kind), (gram.shape, jnp.float32)],
        [
            pltpu.VMEM((chips - 1, comps, cols, group, depth), kind),
            pltpu.VMEM((2 * everyone, everyone), jnp.float32),
        ],
        "last_stage",
    )


def product(a, b):
    return jnp.dot(a, b, preferred_element_type=jnp.float32)


def whiten_kernel(count, gram, *refs):
    pieces, (out, slots, sems) = refs[:-3], refs[-3:]
    everyone = 2 * gram.shape[0]
    comps, cols, depth = pieces[0].shape[0], pieces[0].shape[2], pieces[0].shape[4]
    pitch = slots.shape[1] // everyone

    def dot(a, b):
        (a_top, a_rest), (b_top, b_rest) = split(a), split(b)
        cross = product(a_top, b_rest) + product(a_rest, b_top)
        return product(a_top, b_top) + cross

    correlation = jnp.concatenate([gram[:, :everyone], gram[:, everyone:]], axis=0) / count
    frob_scale = jnp.sqrt(jnp.sum(correlation * correlation, keepdims=True) + 1e-06)
    approx = correlation / frob_scale
    row = lax.broadcasted_iota(jnp.int32, (everyone, everyone), 0)
    col = lax.broadcasted_iota(jnp.int32, (everyone, everyone), 1)
    diagonal = jnp.where(row == col, 3.0, 0.0)
    factor = 0.5 * (diagonal - approx)
    inverse = factor
    for _ in range(1, NSITER):
        approx = dot(approx, factor)
        factor = 0.5 * (diagonal - dot(inverse, approx))
        inverse = dot(factor, inverse)
    top, rest = split(inverse / jnp.sqrt(frob_scale))
    left = jnp.concatenate([top, rest], axis=0)
    left = jnp.concatenate([left, left], axis=1)
    slot, copies = 0, []
    planes = sum(piece.shape[1] for piece in pieces)
    order = [1] + list(range(2, planes)) + [0]
    for piece in pieces:
        for index in range(piece.shape[1]):
            plane = plane_at(order.pop(0), planes)
            for comp in range(comps):
                for first in range(0, cols, 2):
                    both = [piece[comp, index, first], piece[comp, index, first + 1]]
                    both = jnp.concatenate(both, axis=1)
                    mixed = product(left, both)
                    mixed = mixed[:everyone] + mixed[everyone:]
                    for sub in range(2):
                        slots[slot, pl.ds(first + sub, everyone, stride=pitch), :] = mixed[
                            :, sub * depth : (sub + 1) * depth
                        ]
                source = slots.reshape(slots.shape[0], everyone, pitch, depth)
                copies.append(
                    pltpu.make_async_copy(
                        source.at[slot, :, pl.ds(0, cols)],
                        out.at[:, comp, plane],
                        sems.at[slot],
                    )
                )
                copies[-1].start()
                slot += 1
    for item in copies:
        item.wait()


def whiten(gram, pieces, count):
    everyone = 2 * gram.shape[0]
    comps, _, cols, _, depth = pieces[0].shape
    planes = sum(piece.shape[1] for piece in pieces)
    pitch = cols + 8 if (cols // 8) % 2 == 0 else cols
    whole = pl.BlockSpec(memory_space=pltpu.VMEM)
    return pl.pallas_call(
        functools.partial(whiten_kernel, count),
        in_specs=[whole] * (1 + len(pieces)),
        out_specs=pl.BlockSpec(memory_space=pl.ANY),
        out_shape=jax.ShapeDtypeStruct((everyone, comps, planes, cols, depth), jnp.float32),
        scratch_shapes=[
            pltpu.VMEM((comps * planes, everyone * pitch, depth), jnp.float32),
            pltpu.SemaphoreType.DMA((comps * planes,)),
        ],
        compiler_params=pltpu.CompilerParams(vmem_limit_bytes=VMEM_BYTES),
        name="whiten",
    )(gram, *pieces)


def to_chip(array, step):
    count = lax.axis_size("snap")
    pairs = [(i, (i + step * CORES) % count) for i in range(count)]
    return lax.ppermute(array, "snap", pairs)


def to_core(array):
    return lax.ppermute(array, "snap", [(i, i ^ 1) for i in range(lax.axis_size("snap"))])


def to_pair(array, first):
    count = lax.axis_size("slab")
    pairs = [(i, i + 1) for i in range(first, count - 1, 2)]
    return lax.ppermute(array, "slab", pairs + [(j, i) for i, j in pairs])


def all_sum(value):
    for axis in ("slab", "snap"):
        count = lax.axis_size(axis)
        if count & (count - 1):
            value = lax.psum(value, axis)
            continue
        while count > 1:
            step = count // 4 if count > 2 else 1
            received = [
                lax.ppermute(value, axis, [(i, i ^ k) for i in range(lax.axis_size(axis))])
                for k in range(step, count, step)
            ]
            value = sum(received, value)
            count = step
    return value


def per_device(flow, large_scale, modulation, metric):
    snap_count = lax.axis_size("snap")
    slab_count = lax.axis_size("slab")
    _, comps, planes, width, depth = flow.shape
    chips = snap_count // CORES
    cols = width // snap_count
    core = lax.rem(lax.axis_index("snap"), CORES)

    def half(array):
        return lax.dynamic_slice_in_dim(array, (1 - core) * cols, cols, 1)

    assert planes >= 2
    own, other, mine, near = pack(flow, large_scale, chips, cols)
    pair = to_pair(own[0], 0)
    outer, arrays = own[1], []
    for step in range(1, chips):
        both = jnp.concatenate([mine[step - 1], to_core(other[step - 1])], axis=3)
        outer, both = lax.optimization_barrier((outer, both))
        here = [to_chip(both[:, slot, 1:-1], step) for slot in range(planes)]
        edge = jnp.stack([both[:, :, 0], both[:, :, -1]], axis=2)
        edge = edge.reshape(comps, 2 * planes, *edge.shape[3:])
        edge, _ = lax.optimization_barrier((edge, here[0]))
        arrays.append((here + [to_chip(edge, step)], to_pair(here[0], 0), to_pair(here[1], 1)))
    away = to_pair(outer, 1)
    pair, away, _ = lax.optimization_barrier((pair, away, [here[:planes] for here, *_ in arrays]))
    sources = own + [near[0], to_core(near[1]), pair, away]
    sources += [to_core(half(pair)), to_core(half(away))]
    early, coef, amplitude = near_stage(modulation, metric, large_scale, sources, chips, cols)
    sources = []
    for here, _, outer_halo in arrays:
        sources += here + [outer_halo]
    far, gram, base = far_stage(coef, amplitude, early, sources, chips)
    sources = [inner_halo for _, inner_halo, _ in arrays]
    last, gram = last_stage(coef, early, gram, base, sources, chips)
    pieces = [far, last]
    return whiten(all_sum(gram), pieces, float(comps * planes * slab_count * width * depth))


def solution(mesh):
    return jax.shard_map(
        per_device,
        mesh=mesh,
        in_specs=(
            P("snap", None, "slab", None, None),
            P(None, "slab", None, None),
            P(),
            P(None, "slab", None, None),
        ),
        out_specs=P(None, None, "slab", "snap", None),
        check_vma=False,
    )
```

```python
import functools

import jax
import jax.numpy as jnp
from jax import lax
from jax.experimental import pallas as pl
from jax.experimental.pallas import tpu as pltpu
from jax.sharding import PartitionSpec as P

NSITER = 6
CORES = 2
VMEM_BYTES = 16 * 1024 * 1024


def whereabouts():
    place = lax.axis_index("snap")
    return lax.div(place, CORES), lax.rem(place, CORES)


def plane_at(slot, planes):
    upper = lax.rem(lax.axis_index("slab"), 2)
    if slot == 0:
        return (1 - upper) * (planes - 1)
    if slot == 1:
        return upper * (planes - 1)
    return slot - 1


def halo_at(slot, planes):
    upper = lax.rem(lax.axis_index("slab"), 2)
    return (1 - upper if slot == 0 else upper) * (planes + 1)


def spread(flat, pitch, snaps, values_of):
    for snap in range(snaps):
        values = values_of(snap)
        flat[pl.ds(snap * pitch, values.shape[0]), :] = values.astype(jnp.float32)

    def column(col):
        return flat[pl.ds(col, snaps, stride=pitch), :].astype(jnp.bfloat16)

    return column


def pack_own_kernel(planes, cols, flow, large, *refs):
    own, (near, flat, near_large, rows, sems) = refs[:-5], refs[-5:]
    snaps, comps, span = flow.shape[0], flow.shape[1], CORES * cols
    chip, core = whereabouts()
    first = pl.multiple_of(chip * span, span)
    copies = {}
    for slot in range(planes):
        for comp in range(comps):
            index = slot * comps + comp
            copies[index] = pltpu.make_async_copy(
                flow.at[:, comp, plane_at(slot, planes), pl.ds(first, span)],
                near.at[index],
                sems.at[index],
            )
            copies[index].start()
    fetch = pltpu.make_async_copy(large, near_large, sems.at[planes * comps])
    fetch.start()
    for slot in range(planes):
        for comp in range(comps):
            index = slot * comps + comp
            copies[index].wait()
            column = spread(flat, span + 1, snaps, lambda snap: near[index, snap])
            for col in range(span):
                own[slot][comp, col] = column(col)
    fetch.wait()
    rows[...] = near_large[...].astype(jnp.float32)
    start = pl.multiple_of(first + core * cols, 8)
    for slot in range(planes):
        for comp in range(comps):
            values = rows[comp, plane_at(slot, planes), pl.ds(start, cols), :]
            if cols % snaps:
                values = jnp.concatenate([values] * (snaps // cols), axis=0)
            for piece in range(values.shape[0] // snaps):
                tile = values[piece * snaps : (piece + 1) * snaps]
                own[slot][comp, span + piece] = tile.astype(jnp.bfloat16)


def pack_windows_kernel(chips, planes, cols, kinds, flow, *refs):
    outs, flat = refs[:-1], refs[-1]
    snaps, width = flow.shape[0], flow.shape[3]
    chip, core = whereabouts()
    for slot in range(planes):
        plane = plane_at(slot, planes)
        column = spread(flat, width + 1, snaps, lambda snap: flow[snap, 0, plane])
        for target, (mine, step) in zip(outs, kinds):
            part = core if mine else 1 - core
            start = lax.rem(chip + step, chips) * (CORES * cols) + part * cols
            left = column(lax.rem(start - 1 + width, width))
            right = column(lax.rem(start + cols, width))
            if mine and step == 0:
                target[0, 2 * slot] = left
                target[0, 2 * slot + 1] = right
                continue
            target[0, slot, 0] = left
            for col in range(cols):
                target[0, slot, col + 1] = column(start + col)
            target[0, slot, cols + 1] = right


def pack(flow, large, chips, cols):
    snaps, comps, planes, width, depth = flow.shape
    extra, span = -(-cols // snaps), CORES * cols
    kind = flow.dtype
    params = pltpu.CompilerParams(vmem_limit_bytes=VMEM_BYTES)
    def windows(kinds, after, name):
        here = flow if after is None else lax.optimization_barrier((flow, after))[0]

        def shape(mine, step):
            edge = mine and step == 0
            return (comps, 2 * planes) if edge else (comps, planes, cols + 2)

        shapes = [shape(*item) + (snaps, depth) for item in kinds]
        specs = [
            pl.BlockSpec((1,) + item[1:], lambda comp, tail=len(item) - 1: (comp,) + (0,) * tail)
            for item in shapes
        ]
        return pl.pallas_call(
            functools.partial(pack_windows_kernel, chips, planes, cols, kinds),
            grid=(comps,),
            in_specs=[
                pl.BlockSpec((snaps, 1, planes, width, depth), lambda comp: (0, comp, 0, 0, 0)),
            ],
            out_specs=specs,
            out_shape=[jax.ShapeDtypeStruct(item, kind) for item in shapes],
            scratch_shapes=[pltpu.VMEM(((snaps + 1) * (width + 1), depth), jnp.float32)],
            compiler_params=params,
            name=name,
        )(here)

    away = range(1, chips)
    other = windows([(False, step) for step in away], None, "pack_other")
    lengths = [span + extra] + [span + extra] * (planes - 1)
    own = pl.pallas_call(
        functools.partial(pack_own_kernel, planes, cols),
        in_specs=[pl.BlockSpec(memory_space=pltpu.HBM)] * 2,
        out_specs=[pl.BlockSpec(memory_space=pltpu.VMEM)] * planes,
        out_shape=[jax.ShapeDtypeStruct((comps, item, snaps, depth), kind) for item in lengths],
        scratch_shapes=[
            pltpu.VMEM((planes * comps, snaps, span, depth), kind),
            pltpu.VMEM(((snaps + 1) * (span + 1), depth), jnp.float32),
            pltpu.VMEM(large.shape, kind),
            pltpu.VMEM(large.shape, jnp.float32),
            pltpu.SemaphoreType.DMA((planes * comps + 1,)),
        ],
        compiler_params=pltpu.CompilerParams(vmem_limit_bytes=VMEM_BYTES),
        name="pack_own",
    )(lax.optimization_barrier((flow, other[0]))[0], large)
    mine = windows([(True, step) for step in away], own[0], "pack_mine")
    near = windows([(True, 0), (False, 0)], mine[0], "pack_near")
    return list(own), list(other), list(mine), list(near)


def coefficients(wide, metric, large, coef, first):
    comps, (_, planes, cols, depth) = 3, metric.shape
    width = large.shape[2]

    def rolled(comp, plane):
        values = large[comp, plane].astype(jnp.float32)
        return pltpu.roll(values, lax.rem(width + 1 - first, width), 0)

    def at(comp, plane):
        if 0 <= plane < planes:
            return rolled(comp, plane)[1 : cols + 1]
        side = 0 if plane < 0 else 1
        rows = [wide[side, comp, piece] for piece in range(wide.shape[2])]
        return jnp.concatenate(rows, axis=0).astype(jnp.float32)[:cols]

    for plane in range(planes):
        half_x, half_shear, half_y, half_z = [0.5 * metric[k, plane] for k in range(4)]
        step_y = [at(comp, plane + 1) - at(comp, plane - 1) for comp in range(comps)]
        step_z = [along_z(at(comp, plane)) for comp in range(2)]
        after = [rolled(comp, plane)[2 : cols + 2] for comp in (1, 2)]
        before = [rolled(comp, plane)[:cols] for comp in (1, 2)]
        rows = [
            half_x,
            half_shear,
            half_y,
            half_z,
            half_y * step_y[2] - half_z * step_z[1],
            half_z * step_z[0] - half_shear * step_y[2],
            half_shear * step_y[1] - half_y * step_y[0],
            half_x * after[0],
            half_x * before[0],
            half_x * after[1],
            half_x * before[1],
        ]
        for index, value in enumerate(rows):
            coef[plane, index] = value


def along_z(values):
    depth = values.shape[-1]
    return pltpu.roll(values, depth - 1, 1) - pltpu.roll(values, 1, 1)


def curl(get, row, mods, plane, col, inner=None):
    def value(comp, plane_at, col_at):
        return get(comp, plane_at, col_at).astype(jnp.float32)

    gx, shear, gy, gz, ax, ay, az, v_after, v_before, w_after, w_before = row
    mod_before, mod_here, mod_after = mods
    if inner is None:
        steps = [value(k, plane + 1, col) - value(k, plane - 1, col) for k in range(3)]
    else:
        steps = [-value(k, inner, col) for k in range(3)]
    dy_u, dy_v, dy_w = steps
    dz_u, dz_v = [along_z(value(k, plane, col)) for k in range(2)]
    dx_v, dx_w = [value(k, plane, col + 1) - value(k, plane, col - 1) for k in (1, 2)]
    around_x = gy * dy_w - gz * dz_v + mod_here * ax
    around_y = (
        gz * dz_u - gx * dx_w - shear * dy_w + mod_here * ay
        - (mod_after * w_after - mod_before * w_before)
    )
    around_z = (
        gx * dx_v + shear * dy_v - gy * dy_u + mod_here * az
        + (mod_after * v_after - mod_before * v_before)
    )
    return around_x, around_y, around_z


def split(value):
    top = value.astype(jnp.bfloat16)
    return top, (value - top.astype(jnp.float32)).astype(jnp.bfloat16)


def rows_of(chips, step, part, snaps):
    chip, core = whereabouts()
    owner = lax.rem(chip + chips - step, chips) * CORES + (1 - core if part else core)
    return pl.multiple_of(owner * snaps, snaps)


def metric_rows(coef, plane, col, indices, snaps):
    depth = coef.shape[3]
    return [
        jnp.broadcast_to(coef[plane, index, pl.ds(col, 1), :], (snaps, depth)) for index in indices
    ]


def curls(chips, field, steps, coef, amplitude, plane, cols, snaps, store, upper=None):
    for col in range(cols):
        row = metric_rows(coef, plane, col, range(11), snaps)
        inner = None
        if upper is not None:
            sign = (1 - 2 * upper).astype(jnp.float32)
            row[1], row[2] = row[1] * sign, row[2] * sign
            inner = plane + 2 * upper
        for step in steps:
            for part in range(CORES):
                start = rows_of(chips, step, part, snaps)
                mods = [amplitude[col + k, pl.ds(start, snaps), :] for k in range(3)]
                get = functools.partial(field, step, part)
                values = curl(get, row, mods, plane + 1, col + 1, inner)
                for comp, value in enumerate(values):
                    store(comp, col, step, part, start, value)


def near_kernel(chips, planes, modulation, metric, large, *refs):
    own, (edge, other, pair, away, pair_other, away_other) = refs[:planes], refs[planes : planes + 6]
    early, coef, amplitude, mod, metric_mine, large_mine, wide, field, sem = refs[planes + 6 :]
    snaps, cols = early.shape[5], early.shape[2]
    extra = wide.shape[2]
    chip, core = whereabouts()
    first = pl.multiple_of((chip * CORES + core) * cols, 8)
    middle, left, right = pl.ds(1, cols), pl.ds(0, 1), pl.ds(cols + 1, 1)
    mine = pl.ds(core * cols, cols)
    moves = [
        (modulation, mod),
        (metric.at[:, :, pl.ds(first, cols)], metric_mine),
        (large, large_mine),
    ]
    for slot in range(planes):
        plane = plane_at(slot, planes) + 1
        moves += [
            (own[slot].at[:, mine], field.at[0, plane, :, middle]),
            (edge.at[:, pl.ds(2 * slot, 1)], field.at[0, plane, :, left]),
            (edge.at[:, pl.ds(2 * slot + 1, 1)], field.at[0, plane, :, right]),
            (other.at[:, slot], field.at[1, plane]),
        ]
    for slot, (close, far) in enumerate(((pair, pair_other), (away, away_other))):
        halo = halo_at(slot, planes)
        moves += [
            (close.at[:, mine], field.at[0, halo, :, middle]),
            (far, field.at[1, halo, :, middle]),
            (close.at[:, pl.ds(CORES * cols, extra)], wide.at[jnp.minimum(halo, 1)]),
        ]
    fetch_all(moves, sem.at[0])

    doubled = jnp.concatenate([mod[...], mod[...]], axis=1)
    doubled = pltpu.roll(doubled, lax.rem(doubled.shape[1] + 1 - first, doubled.shape[1]), 1)
    for col in range(cols + 2):
        amplitude[col] = jnp.broadcast_to(doubled[:, col : col + 1], amplitude.shape[1:])
    coefficients(wide, metric_mine, large_mine, coef, first)

    def tile(step, part, comp, plane, col):
        return field[part, plane, comp, col]

    for slot in range(planes):

        def store(comp, col, step, part, start, value):
            for level, half in enumerate(split(value)):
                early[comp, slot, col, level, part] = half

        curls(chips, tile, [0], coef, amplitude, plane_at(slot, planes), cols, snaps, store)


def fetch_all(moves, sem):
    copies = [pltpu.make_async_copy(source, target, sem) for source, target in moves]
    for item in copies:
        item.start()
    for item in copies:
        item.wait()


def near_stage(modulation, metric, large, sources, chips, cols):
    everyone, _ = modulation.shape
    comps, planes, _, depth = large.shape
    snaps = everyone // (chips * CORES)
    extra = sources[1].shape[1] - CORES * cols
    whole = pl.BlockSpec(memory_space=pltpu.VMEM)
    return pl.pallas_call(
        functools.partial(near_kernel, chips, planes),
        in_specs=[pl.BlockSpec(memory_space=pl.ANY)] * (3 + len(sources)),
        out_specs=[whole] * 3,
        out_shape=[
            jax.ShapeDtypeStruct((comps, planes, cols, 2, CORES, snaps, depth), jnp.bfloat16),
            jax.ShapeDtypeStruct((planes, 11, cols, depth), jnp.float32),
            jax.ShapeDtypeStruct((cols + 2, everyone, depth), jnp.float32),
        ],
        scratch_shapes=[
            pltpu.VMEM(modulation.shape, modulation.dtype),
            pltpu.VMEM((4, planes, cols, depth), metric.dtype),
            pltpu.VMEM(large.shape, large.dtype),
            pltpu.VMEM((2, comps, extra, snaps, depth), large.dtype),
            pltpu.VMEM((CORES, planes + 2, comps, cols + 2, snaps, depth), large.dtype),
            pltpu.SemaphoreType.DMA((1,)),
        ],
        compiler_params=pltpu.CompilerParams(vmem_limit_bytes=VMEM_BYTES),
        cost_estimate=pl.CostEstimate(flops=0, bytes_accessed=8 << 20, transcendentals=0),
        name="near_stage",
    )(modulation, metric, large, *sources)


def put(parts, index, comp, col, start, halves):
    everyone = parts.shape[3] // 2
    for level, half in enumerate(halves):
        rows = pl.ds(start + level * everyone, half.shape[0])
        parts[comp, index, col, rows, :] = half


def put_early(chips, early, slot, parts, index):
    cols, snaps = early.shape[2], early.shape[5]
    for part in range(CORES):
        start = rows_of(chips, 0, part, snaps)
        for comp in range(3):
            for col in range(cols):
                halves = [early[comp, slot, col, level, part] for level in range(2)]
                put(parts, index, comp, col, start, halves)


def add_products(parts, index, total):
    for comp in range(3):
        columns = [parts[comp, index, col] for col in range(parts.shape[2])]
        both = jnp.concatenate(columns, axis=1)
        total[...] += lax.dot_general(
            both,
            both[: total.shape[1]],
            (((1,), (1,)), ((), ())),
            preferred_element_type=jnp.float32,
        )


def folded(total):
    everyone = total.shape[1]
    cross = total[everyone:]
    whole = total[:everyone] + (cross + cross.T)
    return jnp.concatenate([whole[: everyone // 2], whole[everyone // 2 :]], axis=1)


def far_kernel(chips, planes, coef, amplitude, early, *refs):
    sources, (parts, gram, base, field, total, sem) = list(refs[:-6]), refs[-6:]
    cols, snaps = early.shape[2], early.shape[5]
    middle, left, right = pl.ds(1, cols), pl.ds(0, 1), pl.ds(cols + 1, 1)
    moves = []
    for step in range(1, chips):
        own = [sources.pop(0) for _ in range(planes)]
        edge, beyond = sources.pop(0), sources.pop(0)
        for slot in range(planes):
            target = field.at[step - 1, plane_at(slot, planes) + 1]
            moves += [
                (own[slot], target.at[:, middle]),
                (edge.at[:, pl.ds(2 * slot, 1)], target.at[:, left]),
                (edge.at[:, pl.ds(2 * slot + 1, 1)], target.at[:, right]),
            ]
        moves.append((beyond, field.at[step - 1, halo_at(1, planes), :, middle]))
    fetch_all(moves, sem.at[0])

    def tile(step, part, comp, plane, col):
        return field[step - 1, plane, comp, col, part * snaps : (part + 1) * snaps]

    total[...] = jnp.zeros_like(total)
    steps = range(1, chips)
    for index, slot in enumerate(range(1, planes)):

        def store(comp, col, step, part, start, value):
            put(parts, index, comp, col, start, split(value))

        put_early(chips, early, slot, parts, index)
        plane = plane_at(slot, planes)
        curls(chips, tile, steps, coef, amplitude, plane, cols, snaps, store)
        add_products(parts, index, total)
    gram[...] = folded(total)

    def store(comp, col, step, part, start, value):
        base[comp, step - 1, col, part * snaps : (part + 1) * snaps, :] = value

    upper = lax.rem(lax.axis_index("slab"), 2)
    plane = plane_at(0, planes)
    curls(chips, tile, steps, coef, amplitude, plane, cols, snaps, store, upper)


def last_kernel(chips, planes, coef, early, before, base, *refs):
    sources, (parts, gram, beyond, total, sem) = refs[:-5], refs[-5:]
    cols, snaps = early.shape[2], early.shape[5]
    fetch_all([(source, beyond.at[k]) for k, source in enumerate(sources)], sem.at[0])
    put_early(chips, early, 0, parts, 0)
    upper = lax.rem(lax.axis_index("slab"), 2)
    sign = (1 - 2 * upper).astype(jnp.float32)
    plane = plane_at(0, planes)
    for col in range(cols):
        shear, gy = [row * sign for row in metric_rows(coef, plane, col, (1, 2), snaps)]
        for step in range(1, chips):
            for part in range(CORES):
                rows = slice(part * snaps, (part + 1) * snaps)
                u, v, w = [beyond[step - 1, k, col, rows].astype(jnp.float32) for k in range(3)]
                added = (gy * w, -(shear * w), shear * v - gy * u)
                start = rows_of(chips, step, part, snaps)
                for comp in range(3):
                    value = base[comp, step - 1, col, rows, :] + added[comp]
                    put(parts, 0, comp, col, start, split(value))
    total[...] = jnp.zeros_like(total)
    add_products(parts, 0, total)
    gram[...] = before[...] + folded(total)


def stage(kernel, wholes, sources, outs, scratch, name):
    whole = pl.BlockSpec(memory_space=pltpu.VMEM)
    return pl.pallas_call(
        kernel,
        in_specs=[whole] * len(wholes) + [pl.BlockSpec(memory_space=pl.ANY)] * len(sources),
        out_specs=[whole] * len(outs),
        out_shape=[jax.ShapeDtypeStruct(*item) for item in outs],
        scratch_shapes=scratch + [pltpu.SemaphoreType.DMA((1,))],
        compiler_params=pltpu.CompilerParams(vmem_limit_bytes=VMEM_BYTES),
        cost_estimate=pl.CostEstimate(flops=0, bytes_accessed=8 << 20, transcendentals=0),
        name=name,
    )(*wholes, *sources)


def far_stage(coef, amplitude, early, sources, chips):
    comps, planes, cols, _, _, snaps, depth = early.shape
    group, everyone = CORES * snaps, snaps * chips * CORES
    kind = jnp.bfloat16
    return stage(
        functools.partial(far_kernel, chips, planes),
        [coef, amplitude, early],
        sources,
        [
            ((comps, planes - 1, cols, 2 * everyone, depth), kind),
            ((everyone // 2, 2 * everyone), jnp.float32),
            ((comps, chips - 1, cols, group, depth), jnp.float32),
        ],
        [
            pltpu.VMEM((chips - 1, planes + 2, comps, cols + 2, group, depth), kind),
            pltpu.VMEM((2 * everyone, everyone), jnp.float32),
        ],
        "far_stage",
    )


def last_stage(coef, early, gram, base, sources, chips):
    comps, planes, cols, _, _, snaps, depth = early.shape
    group, everyone = CORES * snaps, snaps * chips * CORES
    kind = jnp.bfloat16
    return stage(
        functools.partial(last_kernel, chips, planes),
        [coef, early, gram, base],
        sources,
        [((comps, 1, cols, 2 * everyone, depth), kind), (gram.shape, jnp.float32)],
        [
            pltpu.VMEM((chips - 1, comps, cols, group, depth), kind),
            pltpu.VMEM((2 * everyone, everyone), jnp.float32),
        ],
        "last_stage",
    )


def product(a, b):
    return jnp.dot(a, b, preferred_element_type=jnp.float32)


def whiten_kernel(count, gram, *refs):
    pieces, (out, slots, sems) = refs[:-3], refs[-3:]
    everyone = 2 * gram.shape[0]
    comps, cols, depth = pieces[0].shape[0], pieces[0].shape[2], pieces[0].shape[4]
    pitch = slots.shape[1] // (everyone + 1)

    def dot(a, b):
        (a_top, a_rest), (b_top, b_rest) = split(a), split(b)
        cross = product(a_top, b_rest) + product(a_rest, b_top)
        return product(a_top, b_top) + cross

    correlation = jnp.concatenate([gram[:, :everyone], gram[:, everyone:]], axis=0) / count
    frob_scale = jnp.sqrt(jnp.sum(correlation * correlation, keepdims=True) + 1e-06)
    approx = correlation / frob_scale
    row = lax.broadcasted_iota(jnp.int32, (everyone, everyone), 0)
    col = lax.broadcasted_iota(jnp.int32, (everyone, everyone), 1)
    diagonal = jnp.where(row == col, 3.0, 0.0)
    factor = 0.5 * (diagonal - approx)
    inverse = factor
    for _ in range(1, NSITER):
        approx = dot(approx, factor)
        factor = 0.5 * (diagonal - dot(inverse, approx))
        inverse = dot(factor, inverse)
    top, rest = split(inverse / jnp.sqrt(frob_scale))
    left = jnp.concatenate([top, rest], axis=0)
    left = jnp.concatenate([left, left], axis=1)
    slot, copies = 0, []
    planes = sum(piece.shape[1] for piece in pieces)
    order = [1] + list(range(2, planes)) + [0]
    for piece in pieces:
        for index in range(piece.shape[1]):
            plane = plane_at(order.pop(0), planes)
            for comp in range(comps):
                for first in range(0, cols, 2):
                    both = [piece[comp, index, first], piece[comp, index, first + 1]]
                    both = jnp.concatenate(both, axis=1)
                    mixed = product(left, both)
                    mixed = mixed[:everyone] + mixed[everyone:]
                    for sub in range(2):
                        slots[slot, pl.ds(first + sub, everyone, stride=pitch), :] = mixed[
                            :, sub * depth : (sub + 1) * depth
                        ]
                source = slots.reshape(slots.shape[0], everyone + 1, pitch, depth)
                copies.append(
                    pltpu.make_async_copy(
                        source.at[slot, pl.ds(0, everyone), pl.ds(0, cols)],
                        out.at[:, comp, plane],
                        sems.at[slot],
                    )
                )
                copies[-1].start()
                slot += 1
    for item in copies:
        item.wait()


def whiten(gram, pieces, count):
    everyone = 2 * gram.shape[0]
    comps, _, cols, _, depth = pieces[0].shape
    planes = sum(piece.shape[1] for piece in pieces)
    pitch = cols + 8 if (cols // 8) % 2 == 0 else cols
    whole = pl.BlockSpec(memory_space=pltpu.VMEM)
    return pl.pallas_call(
        functools.partial(whiten_kernel, count),
        in_specs=[whole] * (1 + len(pieces)),
        out_specs=pl.BlockSpec(memory_space=pl.ANY),
        out_shape=jax.ShapeDtypeStruct((everyone, comps, planes, cols, depth), jnp.float32),
        scratch_shapes=[
            pltpu.VMEM((comps * planes, (everyone + 1) * pitch, depth), jnp.float32),
            pltpu.SemaphoreType.DMA((comps * planes,)),
        ],
        compiler_params=pltpu.CompilerParams(vmem_limit_bytes=VMEM_BYTES),
        name="whiten",
    )(gram, *pieces)


def to_chip(array, step):
    count = lax.axis_size("snap")
    pairs = [(i, (i + step * CORES) % count) for i in range(count)]
    return lax.ppermute(array, "snap", pairs)


def to_core(array):
    return lax.ppermute(array, "snap", [(i, i ^ 1) for i in range(lax.axis_size("snap"))])


def to_pair(array, first):
    count = lax.axis_size("slab")
    pairs = [(i, i + 1) for i in range(first, count - 1, 2)]
    return lax.ppermute(array, "slab", pairs + [(j, i) for i, j in pairs])


def all_sum(value):
    for axis in ("slab", "snap"):
        count = lax.axis_size(axis)
        if count & (count - 1):
            value = lax.psum(value, axis)
            continue
        while count > 1:
            step = count // 4 if count > 2 else 1
            received = [
                lax.ppermute(value, axis, [(i, i ^ k) for i in range(lax.axis_size(axis))])
                for k in range(step, count, step)
            ]
            value = sum(received, value)
            count = step
    return value


def per_device(flow, large_scale, modulation, metric):
    snap_count = lax.axis_size("snap")
    slab_count = lax.axis_size("slab")
    _, comps, planes, width, depth = flow.shape
    chips = snap_count // CORES
    cols = width // snap_count
    core = lax.rem(lax.axis_index("snap"), CORES)

    def half(array):
        return lax.dynamic_slice_in_dim(array, (1 - core) * cols, cols, 1)

    assert planes >= 2
    own, other, mine, near = pack(flow, large_scale, chips, cols)
    pair = to_pair(own[0], 0)
    outer, arrays = own[1], []
    for step in range(1, chips):
        both = jnp.concatenate([mine[step - 1], to_core(other[step - 1])], axis=3)
        outer, both = lax.optimization_barrier((outer, both))
        here = [to_chip(both[:, slot, 1:-1], step) for slot in range(planes)]
        edge = jnp.stack([both[:, :, 0], both[:, :, -1]], axis=2)
        edge = edge.reshape(comps, 2 * planes, *edge.shape[3:])
        edge, _ = lax.optimization_barrier((edge, here[0]))
        arrays.append((here + [to_chip(edge, step)], to_pair(here[0], 0), to_pair(here[1], 1)))
    away = to_pair(outer, 1)
    pair, away, _ = lax.optimization_barrier((pair, away, [here[:planes] for here, *_ in arrays]))
    sources = own + [near[0], to_core(near[1]), pair, away]
    sources += [to_core(half(pair)), to_core(half(away))]
    early, coef, amplitude = near_stage(modulation, metric, large_scale, sources, chips, cols)
    sources = []
    for here, _, outer_halo in arrays:
        sources += here + [outer_halo]
    far, gram, base = far_stage(coef, amplitude, early, sources, chips)
    sources = [inner_halo for _, inner_halo, _ in arrays]
    last, gram = last_stage(coef, early, gram, base, sources, chips)
    pieces = [far, last]
    return whiten(all_sum(gram), pieces, float(comps * planes * slab_count * width * depth))


def solution(mesh):
    return jax.shard_map(
        per_device,
        mesh=mesh,
        in_specs=(
            P("snap", None, "slab", None, None),
            P(None, "slab", None, None),
            P(),
            P(None, "slab", None, None),
        ),
        out_specs=P(None, None, "slab", "snap", None),
        check_vma=False,
    )
```
